32 devices in a mesh: slab: 4 (over y, x), brick: 8 (over z, core).
Axes of the slice: x: 2, y: 2, z: 4, core: 2. Of those that a mesh axis runs over, the one named last changes fastest.
Arguments:
- verts: float32 [32768, 3, 128], P(('slab', 'brick')), may hold values from -4.2 to 4.2
- stiffness: float32 [32768, 128], P(('slab', 'brick')), may hold values from 0.2 to 2
- local_pairs: int32 [32, 2, 256], P(('slab', 'brick')), may hold values from 0 to 1023, as said below
- border_pick: int32 [32, 128], P(('slab', 'brick')), may hold values from 0 to 1023
- recv_src: int32 [32, 8, 8], P(('slab', 'brick')), may hold values from 0 to 127
- recv_pair: int32 [32, 8, 8], P(('slab', 'brick')), may hold values from -1 to 1023, as said below
- face_pick: int32 [32, 2, 64], P(('slab', 'brick')), may hold values from 0 to 1023
- face_pair: int32 [32, 2, 64], P(('slab', 'brick')), may hold values from -1 to 1023, as said below
Outputs:
- membrane_force: float32 [32768, 3, 128], P(('slab', 'brick'))
The draws below stay inside these ranges and needn't reach their ends.
Inputs may be any that keep to these rules, and one draw needn't show every extreme that they name: `local_pairs`: the two rows of a pair name different patches. `recv_pair`: -1 marks an empty slot; the slots for a device's own brick are empty. `face_pair`: -1 marks an empty slot.
All inputs are finite; a program needn't handle non-finite values.
Results may differ from the reference program's by a relative error of at most 0.0001.
Values sent between devices are 32-bit elements; how exact they have to be, the bound alone decides.
No kernel may reach another device: no remote copies, remote signals or barrier semaphores. Data moves between devices by JAX's collectives and lax.ppermute only.
A program may use at most 128 MiB of HBM per device.

```python
import math
import jax
import jax.numpy as jnp
from jax import lax

NV = 128
PD = 1024
S = 8
B = 128
F = 64
LP = 256
NPATCH = 32768
N_SLAB = 4
N_BRICK = 8
DEVICES = 32


def draw_local_pairs(key, part):
    key_one, key_two = jax.random.split(jax.random.fold_in(key, 11))
    pushed_side = jax.random.randint(key_one, (DEVICES, 1, LP), 0, PD, dtype=jnp.int32)
    offsets = jax.random.randint(key_two, (DEVICES, 1, LP), 1, PD, dtype=jnp.int32)
    pushing_side = (pushed_side + offsets) % PD
    return jnp.concatenate([pushed_side, pushing_side], axis=1)


def busy_slots(key, shape):
    key_one, key_two, key_three = jax.random.split(key, 3)
    levels = jnp.array([1, 2, 4, 8], dtype=jnp.int32)
    level = levels[jax.random.randint(key_one, (shape[0], 1, 1), 0, 4, dtype=jnp.int32)]
    taken = jax.random.randint(key_two, shape, 0, 8, dtype=jnp.int32) < level
    values = jax.random.randint(key_three, shape, 0, PD, dtype=jnp.int32)
    return jnp.where(taken, values, -1)


def draw_recv_pair(key, part):
    slots = busy_slots(jax.random.fold_in(key, 23), (DEVICES, N_BRICK, S))
    own_brick = jnp.arange(DEVICES, dtype=jnp.int32) % N_BRICK
    same = own_brick[:, None, None] == jnp.arange(N_BRICK, dtype=jnp.int32)[None, :, None]
    return jnp.where(same, -1, slots)


def draw_face_pair(key, part):
    return busy_slots(jax.random.fold_in(key, 37), (DEVICES, 2, F))


def plant(values, own_key, least, top_value):
    shape = values.shape
    place = [jax.random.randint(jax.random.fold_in(own_key, axis), (), 0, shape[axis]) for axis in range(len(shape))]
    values = values.at[tuple(place)].set(least)
    longest = shape.index(max(shape))
    place[longest] = (place[longest] + 1) % shape[longest]
    return values.at[tuple(place)].set(top_value)


def block_levels(rng, dims, cuts, smallest, high):
    loudness, own = 1.0, jax.random.fold_in(rng, 6)
    for dim, blocks in cuts:
        draws = jnp.exp(jax.random.uniform(jax.random.fold_in(own, dim), (blocks,), jnp.float32, smallest / len(cuts), high / len(cuts)))
        loudness = loudness * jnp.repeat(draws, dims[dim] // blocks).reshape([-1 if axis == dim else 1 for axis in range(len(dims))])
    return loudness


def bell_draw(rng, extent, spread, most, cuts=(), held_as=jnp.bfloat16):
    level = block_levels(rng, extent, cuts, -0.22, 0.18) if cuts else 1.0
    values = jax.random.normal(rng, extent, jnp.float32) * spread * level
    return jnp.minimum(jnp.maximum(values, -most), most).astype(held_as)


def setup_inputs(seed: int = 0) -> dict:
    seeds = jax.random.split(jax.random.key(seed), 9)
    return {
        "verts": bell_draw(seeds[0], (NPATCH, 3, NV), 0.7, 4.2, ((0, 32),), jnp.float32),
        "stiffness": jnp.clip(jnp.exp(math.log(2.0) - 2.3025851 * jax.random.uniform(seeds[1], (NPATCH, NV), jnp.float32) ** block_levels(seeds[1], (NPATCH, NV), ((0, 32),), -0.2, 0.2)), 0.2, 2.0),
        "local_pairs": draw_local_pairs(jax.random.fold_in(seeds[8], 71), 0),
        "border_pick": plant(jax.random.randint(seeds[3], (DEVICES, B), 0, PD), jax.random.fold_in(seeds[3], 1), 0, PD - 1).astype(jnp.int32),
        "recv_src": plant(jax.random.randint(seeds[4], (DEVICES, N_BRICK, S), 0, B), jax.random.fold_in(seeds[4], 1), 0, B - 1).astype(jnp.int32),
        "recv_pair": draw_recv_pair(jax.random.fold_in(seeds[8], 71), 0),
        "face_pick": plant(jax.random.randint(seeds[6], (DEVICES, 2, F), 0, PD), jax.random.fold_in(seeds[6], 1), 0, PD - 1).astype(jnp.int32),
        "face_pair": draw_face_pair(jax.random.fold_in(seeds[8], 71), 0),
    }


highest = lax.Precision.HIGHEST


def centroids(points):
    return (points + jnp.roll(points, -1, axis=-1) + jnp.roll(points, -2, axis=-1)) / 3.0


def tile_forces(own_points, far_centres, far_weight):
    own_sq = jnp.sum(own_points * own_points, axis=1)
    far_sq = jnp.sum(far_centres * far_centres, axis=1)
    cross_dot = jnp.einsum("pci,pcj->pij", own_points, far_centres, precision=highest)
    dist_sq = own_sq[:, :, None] + far_sq[:, None, :] - 2.0 * cross_dot
    energy = far_weight[:, None, :] * jnp.exp(-0.5 * dist_sq) / own_points.shape[-1]
    row_total = jnp.sum(energy, axis=2)
    col_total = jnp.sum(energy, axis=1)
    pushed = own_points * row_total[:, None, :] - jnp.einsum("pcj,pij->pci", far_centres, energy, precision=highest)
    reaction = far_centres * col_total[:, None, :] - jnp.einsum("pci,pij->pcj", own_points, energy, precision=highest)
    return pushed, reaction


def spread_triangles(pushed, reaction):
    return pushed + (reaction + jnp.roll(reaction, 1, axis=-1) + jnp.roll(reaction, 2, axis=-1)) / 3.0


def reference(verts, stiffness, local_pairs, border_pick, recv_src, recv_pair, face_pick, face_pair):
    device = jnp.arange(DEVICES, dtype=jnp.int32)
    slab_of = device // N_BRICK
    offset = device * PD
    target_loc = (offset[:, None] + local_pairs[:, 0, :]).reshape(-1)
    anchor_loc = (offset[:, None] + local_pairs[:, 1, :]).reshape(-1)
    usable_loc = jnp.ones(target_loc.shape, dtype=verts.dtype)
    source = slab_of[:, None] * N_BRICK + jnp.arange(N_BRICK, dtype=jnp.int32)[None, :]
    anchor_brk = (source[:, :, None] * PD + border_pick[source[:, :, None], recv_src]).reshape(-1)
    target_brk = (offset[:, None, None] + jnp.maximum(recv_pair, 0)).reshape(-1)
    usable_brk = (recv_pair >= 0).astype(verts.dtype).reshape(-1)
    lower_dev = jnp.maximum(device - N_BRICK, 0)
    upper_dev = jnp.minimum(device + N_BRICK, DEVICES - 1)
    anchor_low = (lower_dev[:, None] * PD + face_pick[lower_dev, 1, :]).reshape(-1)
    anchor_up = (upper_dev[:, None] * PD + face_pick[upper_dev, 0, :]).reshape(-1)
    target_low = (offset[:, None] + jnp.maximum(face_pair[:, 0, :], 0)).reshape(-1)
    target_up = (offset[:, None] + jnp.maximum(face_pair[:, 1, :], 0)).reshape(-1)
    usable_low = ((slab_of > 0)[:, None] & (face_pair[:, 0, :] >= 0)).astype(verts.dtype).reshape(-1)
    usable_up = ((slab_of < N_SLAB - 1)[:, None] & (face_pair[:, 1, :] >= 0)).astype(verts.dtype).reshape(-1)
    targets = jnp.concatenate([target_loc, target_brk, target_low, target_up])
    anchors = jnp.concatenate([anchor_loc, anchor_brk, anchor_low, anchor_up])
    usable = jnp.concatenate([usable_loc, usable_brk, usable_low, usable_up])
    total = targets.shape[0]
    block_size = math.gcd(total, 256)
    centres = centroids(verts)

    def step(totals, pieces):
        push_acc, react_acc = totals
        target_idx, anchor_idx, usable_rows = pieces
        weight = stiffness[anchor_idx] * usable_rows[:, None]
        pushed, reaction = tile_forces(verts[target_idx], centres[anchor_idx], weight)
        return (push_acc.at[target_idx].add(pushed), react_acc.at[anchor_idx].add(reaction)), None

    start = (jnp.zeros_like(verts), jnp.zeros_like(verts))
    pieces = (targets.reshape(-1, block_size), anchors.reshape(-1, block_size), usable.reshape(-1, block_size))
    (push_acc, react_acc), ignored = lax.scan(step, start, pieces)
    return spread_triangles(push_acc, react_acc)
```

```python
import functools
import math

import jax
import jax.numpy as jnp
from jax import lax
from jax.experimental import pallas as pl
from jax.experimental.pallas import tpu as pltpu
from jax.sharding import PartitionSpec as P

F32 = jnp.float32
BF16 = jnp.bfloat16
ALPHA = math.sqrt(math.log2(math.e))
OFF = -1.0e5
VMEM_LIMIT = 48 * 1024 * 1024


def rows8(v=None):
    return lax.broadcasted_iota(jnp.int32, (8, 128), 0)


def split3(x):
    high = x.astype(BF16).astype(F32)
    rest = x - high
    mid = rest.astype(BF16).astype(F32)
    return high, mid, rest - mid


def own_block(entry, row):
    return jnp.where(row < 4, entry, jnp.where(row == 7, 1.0, 0.0))


def far_block(entry, row):
    return jnp.where(row < 3, pltpu.roll(entry, 4, 0), jnp.where(row == 3, 1.0, entry))


def energy_pair(owns, fars):
    us = [split3(u) for u in owns]
    ws = [split3(w) for w in fars]
    left = jnp.concatenate([part for h, m, l in us for part in (h, h, m, m, h, l)], axis=0).astype(BF16)
    blocks = [jnp.concatenate([h, m, h, m, l, h], axis=0).astype(BF16) for h, m, l in ws]
    empty = jnp.zeros_like(blocks[0])
    right = jnp.concatenate(
        [
            jnp.concatenate([blocks[0], empty], axis=1),
            jnp.concatenate([empty, blocks[1]], axis=1),
        ],
        axis=0,
    )
    exponent = lax.dot_general(left, right, (((0,), (0,)), ((), ())), preferred_element_type=F32)
    energy = jnp.exp2(exponent)
    high = energy.astype(BF16)
    low = (energy - high.astype(F32)).astype(BF16)
    return high, low, us, ws


def thin(parts):
    stack = jnp.concatenate([part for h, m, l in parts for part in (h, m)], axis=0).astype(BF16)
    return jnp.concatenate([stack, stack], axis=1)


def fold(result):
    first = result[0:8, 0:128] + result[8:16, 0:128]
    second = result[16:24, 128:256] + result[24:32, 128:256]
    return first, second


def pushes(high, low, owns, ws):
    tall = jnp.concatenate(
        [
            jnp.concatenate([high[:, 0:128], low[:, 0:128]], axis=1),
            jnp.concatenate([high[:, 128:256], low[:, 128:256]], axis=1),
        ],
        axis=0,
    )
    result = lax.dot_general(thin(ws), tall, (((1,), (1,)), ((), ())), preferred_element_type=F32)
    return [(own * total[3:4] - total) * (1.0 / ALPHA) for own, total in zip(owns, fold(result))]


def reactions(high, low, fars, us):
    tall = jnp.concatenate([high, low], axis=0)
    result = lax.dot_general(thin(us), tall, (((1,), (0,)), ((), ())), preferred_element_type=F32)
    out = []
    for far, total in zip(fars, fold(result)):
        react = (far * total[7:8] - total) * (1.0 / (3.0 * ALPHA))
        out.append(react + pltpu.roll(react, 1, 1) + pltpu.roll(react, 2, 1))
    return out


def entry_at(ref, index):
    return ref[pl.ds(pl.multiple_of(index * 8, 8), 8), :]


def pack_kernel(
    flags, recv_src, recv_pair, face_pick, face_pair, verts, stiffness,
    table, brick_msg, face_lo, face_hi, coords, sems,
):
    patches = stiffness.shape[0]
    copies = [pltpu.make_async_copy(verts.at[:, c, :], coords.at[c], sems.at[c]) for c in range(3)]
    for copy in copies:
        copy.start()
    for copy in copies:
        copy.wait()

    @pl.loop(0, patches // 8, unroll=4)
    def build(step):
        base = pl.multiple_of(step * 8, 8)
        xs = [coords[c, pl.ds(base, 8), :] * ALPHA for c in range(3)]
        cs = [(x + pltpu.roll(x, 127, 1) + pltpu.roll(x, 126, 1)) * (1.0 / 3.0) for x in xs]
        strength = stiffness[pl.ds(base, 8), :]
        own = -0.5 * (xs[0] * xs[0] + xs[1] * xs[1] + xs[2] * xs[2])
        far = jnp.log2(strength) - 7.0 - 0.5 * (cs[0] * cs[0] + cs[1] * cs[1] + cs[2] * cs[2])
        for k, value in enumerate(xs + [own] + cs + [far]):
            table[pl.ds(step * 64 + k, 8, stride=8), :] = value

    row = rows8()
    bricks, slots = recv_pair.shape[1], recv_pair.shape[2]

    @pl.loop(0, bricks)
    def brick(s):
        for k in range(slots):
            target = recv_pair[0, s, k]
            index = jnp.where(target >= 0, recv_src[0, s, k], -1).astype(F32)
            entry = entry_at(table, jnp.maximum(target, 0))
            slot = s * slots + k
            brick_msg[slot] = jnp.where(row == 3, index, entry)[0:4]

    facing = face_pick.shape[2]

    @pl.loop(0, facing, unroll=4)
    def face(k):
        for side, out in ((0, face_lo), (1, face_hi)):
            target = face_pair[0, side, k]
            usable = (target >= 0) & (flags[side] > 0)
            own = entry_at(table, jnp.maximum(target, 0))
            own = jnp.where((row == 3) & jnp.logical_not(usable), OFF, own)
            out[k] = jnp.where(row < 4, own, entry_at(table, face_pick[0, side, k]))


def local_kernel(local_pairs, table, force):
    force[...] = jnp.zeros_like(force)
    row = rows8()
    count = local_pairs.shape[2]

    @pl.loop(0, count // 4)
    def group(step):
        for half in range(2):
            first = step * 4 + half * 2
            targets = [local_pairs[0, 0, first + k] for k in range(2)]
            anchors = [local_pairs[0, 1, first + k] for k in range(2)]
            owns = [own_block(entry_at(table, t), row) for t in targets]
            fars = [far_block(entry_at(table, a), row) for a in anchors]
            high, low, us, ws = energy_pair(owns, fars)
            push = pushes(high, low, owns, ws)
            react = reactions(high, low, fars, us)
            for k in range(2):
                force[targets[k]] += push[k][0:3]
                force[anchors[k]] += react[k][0:3]


def brick_kernel(border_pick, index, table, message, back, react_out):
    row = rows8()
    count = message.shape[0]

    @pl.loop(0, count // 4)
    def group(step):
        for half in range(2):
            first = step * 4 + half * 2
            owns, fars = [], []
            for k in range(2):
                got = index[first + k]
                anchor = border_pick[0, jnp.maximum(got, 0)]
                x = jnp.concatenate([message[first + k], jnp.zeros((4, 128), F32)], axis=0)
                square = jnp.where(row < 3, x * x, 0.0)
                level = -0.5 * jnp.sum(square, axis=0, keepdims=True) + jnp.where(got >= 0, 0.0, OFF)
                owns.append(jnp.where(row < 3, x, jnp.where(row == 3, level, jnp.where(row == 7, 1.0, 0.0))))
                fars.append(far_block(entry_at(table, anchor), row))
            high, low, us, ws = energy_pair(owns, fars)
            push = pushes(high, low, owns, ws)
            react = reactions(high, low, fars, us)
            for k in range(2):
                back[first + k] = push[k][0:3]
                react_out[first + k] = react[k][0:3]


def face_kernel(flags, sent_lo, got_lo, sent_hi, got_hi, push_out, react_out):
    row = rows8()
    facing = sent_lo.shape[0]
    for side, (sent, got) in enumerate(((sent_lo, got_lo), (sent_hi, got_hi))):

        @pl.when(flags[side] > 0)
        def work():
            @pl.loop(0, facing // 2)
            def group(step):
                first = step * 2
                mine = [sent[first + k] for k in range(2)]
                theirs = [got[first + k] for k in range(2)]
                owns = [own_block(e, row) for e in mine]
                high, low, us, ws = energy_pair(owns, [far_block(e, row) for e in theirs])
                push = pushes(high, low, owns, ws)
                fars = [far_block(e, row) for e in mine]
                high, low, us, ws = energy_pair([own_block(e, row) for e in theirs], fars)
                react = reactions(high, low, fars, us)
                for k in range(2):
                    push_out[side, first + k] = push[k][0:3]
                    react_out[side, first + k] = react[k][0:3]


def final_kernel(
    flags, recv_pair, border_pick, index, face_pick, face_pair,
    force_in, brick_push, brick_react, face_push, face_react, force,
):
    force[...] = force_in[...]
    bricks, slots = recv_pair.shape[1], recv_pair.shape[2]

    @pl.loop(0, bricks)
    def brick(s):
        for k in range(slots):
            slot = s * slots + k
            target = recv_pair[0, s, k]

            @pl.when(target >= 0)
            def add():
                force[target] += brick_push[slot]

            got = index[slot]

            @pl.when(got >= 0)
            def add():
                force[border_pick[0, got]] += brick_react[slot]

    facing = face_pick.shape[2]
    for side in range(2):

        @pl.when(flags[side] > 0)
        def work():
            @pl.loop(0, facing, unroll=2)
            def face(k):
                force[jnp.maximum(face_pair[0, side, k], 0)] += face_push[side, k]
                force[face_pick[0, side, k]] += face_react[side, k]


SMEM = pl.BlockSpec(memory_space=pltpu.SMEM)
VMEM = pl.BlockSpec(memory_space=pltpu.VMEM)
HBM = pl.BlockSpec(memory_space=pl.ANY)


def call(kernel, out, in_specs, out_specs, scratch=(), aliases=None, cost=(0, 0, 0)):
    return pl.pallas_call(
        kernel,
        out_shape=out,
        in_specs=in_specs,
        out_specs=out_specs,
        scratch_shapes=list(scratch),
        input_output_aliases=aliases or {},
        compiler_params=pltpu.CompilerParams(vmem_limit_bytes=VMEM_LIMIT),
        cost_estimate=pl.CostEstimate(flops=cost[0], bytes_accessed=cost[1], transcendentals=cost[2]),
    )


def shape(*dims):
    return jax.ShapeDtypeStruct(dims, F32)


def body(verts, stiffness, local_pairs, border_pick, recv_src, recv_pair, face_pick, face_pair):
    patches = verts.shape[0]
    bricks, slots = recv_pair.shape[1], recv_pair.shape[2]
    facing = face_pick.shape[2]
    count = bricks * slots
    layer = lax.axis_index("slab")
    layers = lax.axis_size("slab")
    flags = jnp.stack([layer > 0, layer < layers - 1]).astype(jnp.int32)

    table, brick_msg, face_lo, face_hi = call(
        pack_kernel,
        (shape(patches * 8, 128), shape(count, 4, 128), shape(facing, 8, 128), shape(facing, 8, 128)),
        [SMEM] * 5 + [HBM, VMEM],
        (VMEM,) * 4,
        scratch=[pltpu.VMEM((3, patches, 128), F32), pltpu.SemaphoreType.DMA((3,))],
        cost=(patches * 128 * 60, patches * 128 * 48, 0),
    )(flags, recv_src, recv_pair, face_pick, face_pair, verts, stiffness)

    arrived = lax.all_to_all(brick_msg, "brick", 0, 0, tiled=True)
    got_hi = lax.ppermute(face_lo, "slab", [(i + 1, i) for i in range(layers - 1)])
    got_lo = lax.ppermute(face_hi, "slab", [(i, i + 1) for i in range(layers - 1)])

    pairs = local_pairs.shape[2]
    tile = 128 * 128
    force = call(
        local_kernel,
        shape(patches, 3, 128),
        [SMEM, VMEM],
        VMEM,
        cost=(pairs * tile * 400, patches * 128 * 44, pairs * tile),
    )(local_pairs, table)

    index = arrived[:, 3, 0].astype(jnp.int32)
    back, brick_react = call(
        brick_kernel,
        (shape(count, 3, 128), shape(count, 3, 128)),
        [SMEM, SMEM, VMEM, VMEM],
        (VMEM, VMEM),
        cost=(count * tile * 400, patches * 128 * 32, count * tile),
    )(border_pick, index, table, arrived)

    brick_push = lax.all_to_all(back, "brick", 0, 0, tiled=True)
    face_push, face_react = call(
        face_kernel,
        (shape(2, facing, 3, 128), shape(2, facing, 3, 128)),
        [SMEM, VMEM, VMEM, VMEM, VMEM],
        (VMEM, VMEM),
        cost=(4 * facing * tile * 400, facing * 128 * 4 * 44, 4 * facing * tile),
    )(flags, face_lo, got_lo, face_hi, got_hi)

    return call(
        final_kernel,
        shape(patches, 3, 128),
        [SMEM] * 6 + [VMEM] * 5,
        VMEM,
        cost=(facing * 128 * 24, patches * 128 * 24, 0),
    )(
        flags, recv_pair, border_pick, index, face_pick, face_pair,
        force, brick_push, brick_react, face_push, face_react,
    )


def solution(mesh):
    placed = (
        P(("slab", "brick"), None, None),
        P(("slab", "brick"), None),
        P(("slab", "brick"), None, None),
        P(("slab", "brick"), None),
        P(("slab", "brick"), None, None),
        P(("slab", "brick"), None, None),
        P(("slab", "brick"), None, None),
        P(("slab", "brick"), None, None),
    )
    return jax.shard_map(
        body,
        mesh=mesh,
        in_specs=placed,
        out_specs=P(("slab", "brick"), None, None),
        check_vma=False,
    )
```

```python
import math

import jax
import jax.numpy as jnp
from jax import lax
from jax.experimental import pallas as pl
from jax.experimental.pallas import tpu as pltpu
from jax.sharding import PartitionSpec as P

F32 = jnp.float32
BF16 = jnp.bfloat16
ALPHA = math.sqrt(math.log2(math.e))
PUSH = 1.0 / ALPHA
REACT = 1.0 / (3.0 * ALPHA)
OFF = -1.0e5
VMEM_LIMIT = 64 * 1024 * 1024
WIDTH = 8
MATMUL = (((1,), (0,)), ((), ()))


def row_index():
    return lax.broadcasted_iota(jnp.int32, (8, 128), 0)


def split3(x):
    high = x.astype(BF16).astype(F32)
    rest = x - high
    mid = rest.astype(BF16).astype(F32)
    return high, mid, rest - mid


def own_block(entry, row):
    return jnp.where(row < 4, entry, jnp.where(row == 7, 1.0, pltpu.roll(entry, 4, 0)))


def far_block(entry, row):
    return jnp.where(row < 3, pltpu.roll(entry, 4, 0), jnp.where(row == 3, 1.0, entry))


def own_rows(parts, row):
    high, mid, low = parts
    one = jnp.where(row == 7, 1.0, 0.0)
    return [high, mid + one, jnp.where(row < 3, high, low) + one]


def far_rows(parts, row):
    high, mid, low = parts
    copy = (row >= 4) & (row < 7)
    return [
        jnp.where(copy, mid, high),
        jnp.where(row < 4, high, mid),
        jnp.where((row >= 3) & (row < 7), high, low),
    ]


def entry_at(ref, index):
    return ref[pl.ds(pl.multiple_of(index * 8, 8), 8), :]


def add_at(ref, index, value):
    ref[pl.ds(pl.multiple_of(index * 8, 8), 8), :] += value


def spread(react):
    return react + pltpu.roll(react, 1, 1) + pltpu.roll(react, 2, 1)


def tile_scratch(width):
    return [
        pltpu.VMEM((2 * width, 128, 48), BF16),
        pltpu.VMEM((2 * width, 48, 256), BF16),
        pltpu.VMEM((2 * width, 32, 128), BF16),
        pltpu.VMEM((2 * width, 128, 256), BF16),
        pltpu.VMEM((2 * width, 128, 256), BF16),
    ]


def run_tiles(start, stop, width, load, finish, scratch):
    lefts, rights, thins, highs, lows = scratch
    row = row_index()

    def prepare(n, slot):
        (far_down, own_down), (own_across, far_across) = load(n)
        left = far_rows(far_down, row) + own_rows(own_down, row)
        empty = [jnp.zeros((8, 128), F32)] * 3
        first = jnp.concatenate(own_rows(own_across, row) + empty, axis=0)
        second = jnp.concatenate(empty + far_rows(far_across, row), axis=0)
        lefts[slot] = jnp.concatenate(left, axis=0).astype(BF16).T
        rights[slot] = jnp.concatenate([first, second], axis=1).astype(BF16)
        thin = jnp.concatenate([far_down[0], far_down[1], own_down[0], own_down[1]], axis=0)
        thins[slot] = thin.astype(BF16)

    def energies(slot):
        energy = jnp.exp2(lax.dot_general(lefts[slot], rights[slot], MATMUL, preferred_element_type=F32))
        high = energy.astype(BF16)
        highs[slot] = high
        lows[slot] = (energy - high.astype(F32)).astype(BF16)

    def totals(slot):
        tall = jnp.concatenate([highs[slot], lows[slot]], axis=0)
        thin = jnp.concatenate([thins[slot], thins[slot]], axis=1)
        result = lax.dot_general(thin, tall, MATMUL, preferred_element_type=F32)
        push = result[0:8, 0:128] + result[8:16, 0:128]
        react = result[16:24, 128:256] + result[24:32, 128:256]
        return push, react

    last = stop - 1
    for q in range(2 * width):
        prepare(jnp.minimum(start + q, last), q)
    for q in range(width):
        energies(q)

    @pl.loop(0, (stop - start) // (2 * width))
    def step(m):
        base = start + m * (2 * width)
        for half in range(2):
            here, there = half * width, (1 - half) * width
            for q in range(width):
                finish(base + here + q, *totals(here + q))
                energies(there + q)
                prepare(jnp.minimum(base + 2 * width + here + q, last), here + q)


def push_of(own, total):
    return (own * total[3:4] - total) * PUSH


def react_of(far, total):
    return spread((far * total[7:8] - total) * REACT)


def width_for(couples):
    return math.gcd(couples, 2 * WIDTH) // 2


def build_table(verts, stiffness, table, first, last):
    @pl.loop(first // 8, last // 8, unroll=4)
    def build(step):
        base = pl.multiple_of(step * 8, 8)
        xs = [verts[c, pl.ds(base, 8), :] * ALPHA for c in range(3)]
        cs = [(x + pltpu.roll(x, 127, 1) + pltpu.roll(x, 126, 1)) * (1.0 / 3.0) for x in xs]
        strength = stiffness[pl.ds(base, 8), :]
        own = -0.5 * (xs[0] * xs[0] + xs[1] * xs[1] + xs[2] * xs[2])
        far = jnp.log2(strength) - 7.0 - 0.5 * (cs[0] * cs[0] + cs[1] * cs[1] + cs[2] * cs[2])
        for k, value in enumerate(xs + [own] + cs + [far]):
            table[pl.ds(step * 64 + k, 8, stride=8), :] = value


def clear_rows(ref):
    @pl.loop(0, ref.shape[0] // 64)
    def clear(n):
        ref[pl.ds(pl.multiple_of(n * 64, 64), 64), :] = jnp.zeros((64, 128), F32)


def message_index(message, index, sem):
    bricks = index.shape[0]
    slots = message.shape[0] // bricks
    return [
        pltpu.make_async_copy(message.at[s * slots, pl.ds(3, 1)], index.at[pl.ds(s, 1)], sem.at[s])
        for s in range(bricks)
    ]


def start_all(copies):
    for copy in copies:
        copy.start()
    return copies


def wait_all(copies):
    for copy in copies:
        copy.wait()


def copies_of(pairs, sem, first=0):
    return [pltpu.make_async_copy(source, target, sem.at[first + n]) for n, (source, target) in enumerate(pairs)]


def pack_kernel(
    border_any, src_any, pair_any, pick_any, facing_any, verts_any, stiffness_any,
    table_any, brick_any, lo_any, hi_any, border_out,
    border_pick, recv_src, recv_pair, face_pick, face_pair, verts, stiffness, table,
    brick_msg, face_lo, face_hi, border, small_sem, large_sem, out_sem, table_sem,
):
    patches = stiffness.shape[0]
    row = row_index()
    parts = table_sem.shape[0]
    rows = patches // parts
    large = []
    for part in range(parts):
        here = pl.ds(part * rows, rows)
        pieces = ((verts_any.at[:, here, :], verts.at[:, here, :]), (stiffness_any.at[here], stiffness.at[here]))
        large.append(start_all(copies_of(pieces, large_sem, 2 * part)))
    small = (
        (border_any, border_pick), (src_any, recv_src), (pair_any, recv_pair),
        (pick_any, face_pick), (facing_any, face_pair),
    )
    small = start_all(copies_of(small, small_sem))
    sends = []
    for part in range(parts):
        wait_all(large[part])
        build_table(verts, stiffness, table, part * rows, (part + 1) * rows)
        here = pl.ds(part * rows * 8, rows * 8)
        sends += start_all([pltpu.make_async_copy(table.at[here], table_any.at[here], table_sem.at[part])])
    wait_all(small)

    @pl.loop(0, border.shape[0] // 8, unroll=8)
    def borders(n):
        border[pl.ds(pl.multiple_of(n * 8, 8), 8), :] = entry_at(table, border_pick[0, n])

    sends += start_all(copies_of([(border, border_out)], out_sem, 3))
    @pl.loop(0, face_lo.shape[0], unroll=4)
    def face(k):
        for side, out in ((0, face_lo), (1, face_hi)):
            target = face_pair[0, side, k]
            level = jnp.where(target >= 0, 0.0, OFF)
            own = entry_at(table, jnp.maximum(target, 0)) + jnp.where(row == 3, level, 0.0)
            out[k] = jnp.where(row < 4, own, entry_at(table, face_pick[0, side, k]))

    sends += start_all(copies_of([(face_lo, lo_any), (face_hi, hi_any)], out_sem, 1))

    lane = lax.broadcasted_iota(jnp.int32, (8, 128), 1)
    bricks, slots = recv_pair.shape[1], recv_pair.shape[2]

    @pl.loop(0, bricks)
    def brick(s):
        index = jnp.full((8, 128), -1.0, F32)
        for k in range(slots):
            wanted = jnp.where(recv_pair[0, s, k] >= 0, recv_src[0, s, k], -1).astype(F32)
            index = jnp.where(lane == k, wanted, index)
        for k in range(slots):
            entry = entry_at(table, jnp.maximum(recv_pair[0, s, k], 0))
            brick_msg[s * slots + k] = jnp.where(row == 3, index, entry)[0:4]

    sends += start_all(copies_of([(brick_msg, brick_any)], out_sem))

    wait_all(sends)


def write_planes(force, planes, planes_out, sem, before=None):
    parts = sem.shape[0]
    rows = planes.shape[1] // parts
    sends = []
    for part in range(parts):

        @pl.loop(part * rows // 8, (part + 1) * rows // 8, unroll=8)
        def unpack(n):
            here = pl.ds(pl.multiple_of(n * 8, 8), 8)
            for c in range(3):
                value = force[pl.ds(n * 64 + c, 8, stride=8), :]
                planes[c, here, :] = value if before is None else planes[c, here, :] + value

        here = pl.ds(part * rows, rows)
        sends += start_all([pltpu.make_async_copy(planes.at[:, here, :], planes_out.at[:, here, :], sem.at[part])])
    wait_all(sends)


def local_kernel(local_any, table_any, planes_out, local_pairs, table, force, planes, sem, plane_sem, *scratch):
    row = row_index()
    copies = start_all(copies_of([(local_any, local_pairs), (table_any, table)], sem))
    clear_rows(force)
    wait_all(copies)

    def load(n):
        own = split3(own_block(entry_at(table, local_pairs[0, 0, n]), row))
        far = split3(far_block(entry_at(table, local_pairs[0, 1, n]), row))
        return (far, own), (own, far)

    def finish(n, push, react):
        target, anchor = local_pairs[0, 0, n], local_pairs[0, 1, n]
        add_at(force, target, push_of(entry_at(table, target), push))
        add_at(force, anchor, react_of(pltpu.roll(entry_at(table, anchor), 4, 0), react))

    pairs = local_pairs.shape[2]
    run_tiles(0, pairs, width_for(pairs), load, finish, scratch)
    write_planes(force, planes, planes_out, plane_sem)


def brick_kernel(border_any, message_any, after_any, back_any, react_any, border, message, back, react_out, index, sem, *scratch):
    row = row_index()
    bricks = index.shape[0]
    count = message.shape[0]
    slots = count // bricks
    copies = message_index(message_any, index, sem)
    copies.append(pltpu.make_async_copy(border_any, border, sem.at[bricks]))
    copies.append(pltpu.make_async_copy(message_any, message, sem.at[bricks + 1]))
    for copy in copies:
        copy.start()
    for copy in copies:
        copy.wait()

    def blocks(n):
        wanted = index[n // slots, n % slots].astype(jnp.int32)
        x = jnp.concatenate([message[n], message[n]], axis=0)
        square = jnp.where(row < 3, x * x, 0.0)
        level = -0.5 * jnp.sum(square, axis=0, keepdims=True) + jnp.where(wanted >= 0, 0.0, OFF)
        own = jnp.where(row == 3, level, jnp.where(row == 7, 1.0, x))
        return own, far_block(entry_at(border, jnp.maximum(wanted, 0)), row)

    def load(n):
        own, far = (split3(block) for block in blocks(n))
        return (far, own), (own, far)

    def finish(n, push, react):
        own, far = blocks(n)
        back[n] = push_of(own, push)[0:4]
        react_out[pl.ds(pl.multiple_of(n * 8, 8), 8), :] = react_of(far, react)

    run_tiles(0, count, width_for(count), load, finish, scratch)
    copies = [
        pltpu.make_async_copy(back, back_any, sem.at[bricks]),
        pltpu.make_async_copy(react_out, react_any, sem.at[bricks + 1]),
    ]
    for copy in copies:
        copy.start()
    for copy in copies:
        copy.wait()


def face_kernel(
    border_any, pick_any, pair_any, message, react_any, planes_in, sent_lo, sent_hi, got_lo, got_hi,
    planes_out, border_pick, face_pick, face_pair, brick_react, planes, force, sent, got, index, sem, index_sem, plane_sem,
    *scratch,
):
    row = row_index()
    facing = face_pick.shape[2]
    bricks = index.shape[0]
    slots = message.shape[0] // bricks
    copies = message_index(message, index, index_sem)
    for side, (mine, theirs) in enumerate(((sent_lo, got_lo), (sent_hi, got_hi))):
        copies.append(pltpu.make_async_copy(mine, sent.at[side], sem.at[side]))
        copies.append(pltpu.make_async_copy(theirs, got.at[side], sem.at[side + 2]))
    for n, (source, target) in enumerate(
        ((border_any, border_pick), (pick_any, face_pick), (pair_any, face_pair), (react_any, brick_react))
    ):
        copies.append(pltpu.make_async_copy(source, target, sem.at[n + 4]))
    before = pltpu.make_async_copy(planes_in, planes, sem.at[8])
    for copy in copies + [before]:
        copy.start()
    clear_rows(force)
    for copy in copies:
        copy.wait()

    @pl.loop(0, bricks)
    def add_bricks(s):
        for k in range(slots):
            anchor = border_pick[0, jnp.maximum(index[s, k].astype(jnp.int32), 0)]
            add_at(force, anchor, entry_at(brick_react, s * slots + k))

    layer = lax.axis_index("slab")
    has_low, has_high = layer > 0, layer < lax.axis_size("slab") - 1

    def load(n):
        side, k = n // facing, n % facing
        mine, theirs = sent[side, k], got[side, k]
        down = split3(far_block(theirs, row)), split3(own_block(theirs, row))
        return down, (split3(own_block(mine, row)), split3(far_block(mine, row)))

    def finish(n, push, react):
        side, k = n // facing, n % facing
        mine = sent[side, k]
        add_at(force, jnp.maximum(face_pair[0, side, k], 0), push_of(mine, push))
        add_at(force, face_pick[0, side, k], react_of(pltpu.roll(mine, 4, 0), react))

    start = jnp.where(has_low, 0, facing)
    stop = jnp.where(has_high, 2 * facing, facing)
    run_tiles(start, stop, width_for(facing), load, finish, scratch)

    before.wait()
    write_planes(force, planes, planes_out, plane_sem, before)


def final_kernel(pair_any, planes_any, push_any, out_any, recv_pair, low, mid, high, brick_push, in_sem, out_sem):
    planes = (low, mid, high)
    small = start_all(copies_of(((push_any, brick_push), (pair_any, recv_pair)), in_sem, 3))
    large = start_all(copies_of([(planes_any.at[c], plane) for c, plane in enumerate(planes)], in_sem))
    bricks, slots = recv_pair.shape[1], recv_pair.shape[2]
    wait_all(small)
    sends = []
    for c, plane in enumerate(planes):
        large[c].wait()

        @pl.loop(0, bricks)
        def brick(s):
            for k in range(slots):
                target = recv_pair[0, s, k]
                push = jnp.where(target >= 0, brick_push[s * slots + k, c:c + 1], 0.0)
                plane[pl.ds(jnp.maximum(target, 0), 1), :] += push

        sends += start_all(copies_of([(plane, out_any.at[c])], out_sem, c))
    wait_all(sends)


HBM = pl.BlockSpec(memory_space=pltpu.HBM)


def call(kernel, out, in_specs, out_specs, scratch, cost):
    return pl.pallas_call(
        kernel,
        out_shape=out,
        in_specs=in_specs,
        out_specs=out_specs,
        scratch_shapes=scratch,
        compiler_params=pltpu.CompilerParams(vmem_limit_bytes=VMEM_LIMIT),
        cost_estimate=pl.CostEstimate(flops=cost[0], bytes_accessed=cost[1], transcendentals=cost[2]),
    )


def shape(*dims):
    return jax.ShapeDtypeStruct(dims, F32)


def body(verts, stiffness, local_pairs, border_pick, recv_src, recv_pair, face_pick, face_pair):
    patches = verts.shape[0]
    bricks, slots = recv_pair.shape[1], recv_pair.shape[2]
    facing = face_pick.shape[2]
    count = bricks * slots
    pairs = local_pairs.shape[2]
    layers = lax.axis_size("slab")
    tile = 128 * 128

    table, brick_msg, face_lo, face_hi, border = call(
        pack_kernel,
        (
            shape(patches * 8, 128), shape(count, 4, 128), shape(facing, 8, 128), shape(facing, 8, 128),
            shape(border_pick.shape[1] * 8, 128),
        ),
        [HBM] * 7,
        (HBM,) * 5,
        scratch=[pltpu.SMEM(array.shape, jnp.int32) for array in (border_pick, recv_src, recv_pair, face_pick, face_pair)]
        + [
            pltpu.VMEM((3, patches, 128), F32),
            pltpu.VMEM((patches, 128), F32),
            pltpu.VMEM((patches * 8, 128), F32),
            pltpu.VMEM((count, 4, 128), F32),
            pltpu.VMEM((facing, 8, 128), F32),
            pltpu.VMEM((facing, 8, 128), F32),
            pltpu.VMEM((border_pick.shape[1] * 8, 128), F32),
        ]
        + [pltpu.SemaphoreType.DMA((n,)) for n in (5, 8, 4, 4)],
        cost=(patches * 128 * 60, patches * 128 * 48, 0),
    )(
        border_pick, recv_src, recv_pair, face_pick, face_pair,
        jnp.transpose(verts, (1, 0, 2)), stiffness,
    )

    arrived = lax.all_to_all(brick_msg, "brick", 0, 0, tiled=True)
    got_hi = lax.ppermute(face_lo, "slab", [((i + 1) % layers, i) for i in range(layers)])
    got_lo = lax.ppermute(face_hi, "slab", [(i, (i + 1) % layers) for i in range(layers)])

    planes = call(
        local_kernel,
        shape(3, patches, 128),
        [HBM] * 2,
        HBM,
        scratch=[
            pltpu.SMEM(local_pairs.shape, jnp.int32),
            pltpu.VMEM((patches * 8, 128), F32),
            pltpu.VMEM((patches * 8, 128), F32),
            pltpu.VMEM((3, patches, 128), F32),
            pltpu.SemaphoreType.DMA((2,)),
            pltpu.SemaphoreType.DMA((4,)),
        ]
        + tile_scratch(WIDTH),
        cost=(pairs * tile * 400, patches * 128 * 48, pairs * tile),
    )(local_pairs, table)

    back, brick_react = call(
        brick_kernel,
        (shape(count, 4, 128), shape(count * 8, 128)),
        [HBM, HBM, HBM],
        (HBM, HBM),
        scratch=[
            pltpu.VMEM(border.shape, F32),
            pltpu.VMEM(arrived.shape, F32),
            pltpu.VMEM((count, 4, 128), F32),
            pltpu.VMEM((count * 8, 128), F32),
            pltpu.SMEM((bricks, 128), F32),
            pltpu.SemaphoreType.DMA((bricks + 2,)),
        ]
        + tile_scratch(WIDTH),
        cost=(count * tile * 400, patches * 128 * 32, count * tile),
    )(border, arrived, planes)

    brick_push = lax.all_to_all(back, "brick", 0, 0, tiled=True)
    planes = call(
        face_kernel,
        shape(3, patches, 128),
        [HBM] * 10,
        HBM,
        scratch=[
            pltpu.SMEM(border_pick.shape, jnp.int32),
            pltpu.SMEM(face_pick.shape, jnp.int32),
            pltpu.SMEM(face_pair.shape, jnp.int32),
            pltpu.VMEM((count * 8, 128), F32),
            pltpu.VMEM((3, patches, 128), F32),
            pltpu.VMEM((patches * 8, 128), F32),
            pltpu.VMEM((2, facing, 8, 128), F32),
            pltpu.VMEM((2, facing, 8, 128), F32),
            pltpu.SMEM((bricks, 128), F32),
            pltpu.SemaphoreType.DMA((9,)),
            pltpu.SemaphoreType.DMA((bricks,)),
            pltpu.SemaphoreType.DMA((4,)),
        ]
        + tile_scratch(WIDTH),
        cost=(4 * facing * tile * 400, patches * 128 * 64, 4 * facing * tile),
    )(border_pick, face_pick, face_pair, arrived, brick_react, planes, face_lo, face_hi, got_lo, got_hi)

    out = call(
        final_kernel,
        shape(3, patches, 128),
        [HBM, HBM, HBM],
        HBM,
        scratch=[pltpu.SMEM(recv_pair.shape, jnp.int32)]
        + [pltpu.VMEM((patches, 128), F32)] * 3
        + [pltpu.VMEM((count, 4, 128), F32), pltpu.SemaphoreType.DMA((5,)), pltpu.SemaphoreType.DMA((3,))],
        cost=(count * 128 * 24, patches * 128 * 24, 0),
    )(recv_pair, planes, brick_push)
    return jnp.transpose(out, (1, 0, 2))


def solution(mesh):
    placed = (
        P(("slab", "brick"), None, None),
        P(("slab", "brick"), None),
        P(("slab", "brick"), None, None),
        P(("slab", "brick"), None),
        P(("slab", "brick"), None, None),
        P(("slab", "brick"), None, None),
        P(("slab", "brick"), None, None),
        P(("slab", "brick"), None, None),
    )
    return jax.shard_map(
        body,
        mesh=mesh,
        in_specs=placed,
        out_specs=P(("slab", "brick"), None, None),
        check_vma=False,
    )
```

```python
import math

import jax
import jax.numpy as jnp
from jax import lax
from jax.experimental import pallas as pl
from jax.experimental.pallas import tpu as pltpu
from jax.sharding import PartitionSpec as P

F32 = jnp.float32
BF16 = jnp.bfloat16
ALPHA = math.sqrt(math.log2(math.e))
PUSH = 1.0 / ALPHA
REACT = 1.0 / (3.0 * ALPHA)
OFF = -1.0e5
VMEM_LIMIT = 64 * 1024 * 1024
WIDTH = 8
MATMUL = (((1,), (0,)), ((), ()))


def row_index():
    return lax.broadcasted_iota(jnp.int32, (8, 128), 0)


def split3(x):
    high = x.astype(BF16).astype(F32)
    rest = x - high
    mid = rest.astype(BF16).astype(F32)
    return high, mid, rest - mid


def own_block(entry, row):
    return jnp.where(row < 4, entry, jnp.where(row == 7, 1.0, pltpu.roll(entry, 4, 0)))


def far_block(entry, row):
    return jnp.where(row < 3, pltpu.roll(entry, 4, 0), jnp.where(row == 3, 1.0, entry))


def own_rows(parts, row):
    high, mid, low = parts
    one = jnp.where(row == 7, 1.0, 0.0)
    return [high, mid + one, jnp.where(row < 3, high, low) + one]


def far_rows(parts, row):
    high, mid, low = parts
    copy = (row >= 4) & (row < 7)
    return [
        jnp.where(copy, mid, high),
        jnp.where(row < 4, high, mid),
        jnp.where((row >= 3) & (row < 7), high, low),
    ]


def entry_at(ref, index):
    return ref[pl.ds(pl.multiple_of(index * 8, 8), 8), :]


def add_at(ref, index, value):
    ref[pl.ds(pl.multiple_of(index * 8, 8), 8), :] += value


def spread(react):
    return react + pltpu.roll(react, 1, 1) + pltpu.roll(react, 2, 1)


def tile_scratch(width):
    return [
        pltpu.VMEM((2 * width, 128, 48), BF16),
        pltpu.VMEM((2 * width, 48, 256), BF16),
        pltpu.VMEM((2 * width, 32, 128), BF16),
        pltpu.VMEM((2 * width, 128, 256), BF16),
        pltpu.VMEM((2 * width, 128, 256), BF16),
        pltpu.VMEM((2 * width, 2, 8, 128), F32),
    ]


def run_tiles(start, stop, width, load, finish, scratch):
    lefts, rights, thins, highs, lows, sums = scratch
    row = row_index()

    def prepare(n, slot):
        (far_down, own_down), (own_across, far_across) = load(n)
        left = far_rows(far_down, row) + own_rows(own_down, row)
        empty = [jnp.zeros((8, 128), F32)] * 3
        first = jnp.concatenate(own_rows(own_across, row) + empty, axis=0)
        second = jnp.concatenate(empty + far_rows(far_across, row), axis=0)
        lefts[slot] = jnp.concatenate(left, axis=0).astype(BF16).T
        rights[slot] = jnp.concatenate([first, second], axis=1).astype(BF16)
        thin = jnp.concatenate([far_down[0], far_down[1], own_down[0], own_down[1]], axis=0)
        thins[slot] = thin.astype(BF16)

    def energies(slot):
        energy = jnp.exp2(lax.dot_general(lefts[slot], rights[slot], MATMUL, preferred_element_type=F32))
        high = energy.astype(BF16)
        highs[slot] = high
        lows[slot] = (energy - high.astype(F32)).astype(BF16)

    def totals(slot):
        tall = jnp.concatenate([highs[slot], lows[slot]], axis=0)
        thin = jnp.concatenate([thins[slot], thins[slot]], axis=1)
        result = lax.dot_general(thin, tall, MATMUL, preferred_element_type=F32)
        push = result[0:8, 0:128] + result[8:16, 0:128]
        react = result[16:24, 128:256] + result[24:32, 128:256]
        return push, react

    last = stop - 1
    for q in range(2 * width):
        prepare(jnp.minimum(start + q, last), q)
    for q in range(width):
        energies(q)

    sums[width:] = jnp.zeros((width, 2, 8, 128), F32)

    @pl.loop(0, (stop - start) // (2 * width))
    def step(m):
        base = start + m * (2 * width)
        for half in range(2):
            here, there = half * width, (1 - half) * width
            for q in range(width):
                finish(jnp.maximum(base + here + q - width, start), sums[there + q, 0], sums[there + q, 1])
                sums[here + q, 0], sums[here + q, 1] = totals(here + q)
                energies(there + q)
                prepare(jnp.minimum(base + 2 * width + here + q, last), here + q)

    for q in range(width):
        finish(stop - width + q, sums[width + q, 0], sums[width + q, 1])


def push_of(own, total):
    return (own * total[3:4] - total) * PUSH


def react_of(far, total):
    return spread((far * total[7:8] - total) * REACT)


def width_for(couples):
    return math.gcd(couples, 2 * WIDTH) // 2


def build_table(verts, stiffness, table, first, last):
    @pl.loop(first // 8, last // 8, unroll=32)
    def build(step):
        base = pl.multiple_of(step * 8, 8)
        xs = [verts[c, pl.ds(base, 8), :] * ALPHA for c in range(3)]
        cs = [(x + pltpu.roll(x, 127, 1) + pltpu.roll(x, 126, 1)) * (1.0 / 3.0) for x in xs]
        strength = stiffness[pl.ds(base, 8), :]
        own = -0.5 * (xs[0] * xs[0] + xs[1] * xs[1] + xs[2] * xs[2])
        far = jnp.log2(strength) - 7.0 - 0.5 * (cs[0] * cs[0] + cs[1] * cs[1] + cs[2] * cs[2])
        for k, value in enumerate(xs + [own] + cs + [far]):
            table[pl.ds(step * 64 + k, 8, stride=8), :] = value


def clear_rows(ref):
    @pl.loop(0, ref.shape[0] // 64, unroll=8)
    def clear(n):
        ref[pl.ds(pl.multiple_of(n * 64, 64), 64), :] = jnp.zeros((64, 128), F32)


def message_index(message, index, sem):
    return pltpu.make_async_copy(message.at[:, 3, :], index, sem)


def start_all(copies):
    for copy in copies:
        copy.start()
    return copies


def wait_all(copies):
    for copy in copies:
        copy.wait()


def copies_of(pairs, sem, first=0):
    return [pltpu.make_async_copy(source, target, sem.at[first + n]) for n, (source, target) in enumerate(pairs)]


def pack_kernel(
    local_any, border_any, src_any, pair_any, pick_any, facing_any, verts_any, stiffness_any,
    near_any, brick_any, lo_any, hi_any, border_out,
    local_pairs, border_pick, recv_src, recv_pair, face_pick, face_pair, verts, stiffness, table, near,
    brick_msg, face_lo, face_hi, border, small_sem, large_sem, out_sem,
):
    patches = stiffness.shape[0]
    row = row_index()
    parts = large_sem.shape[0] // 2
    rows = patches // parts
    large = []
    for part in range(parts):
        here = pl.ds(part * rows, rows)
        pieces = ((verts_any.at[:, here, :], verts.at[:, here, :]), (stiffness_any.at[here], stiffness.at[here]))
        large.append(start_all(copies_of(pieces, large_sem, 2 * part)))
    small = (
        (local_any, local_pairs), (border_any, border_pick), (src_any, recv_src), (pair_any, recv_pair),
        (pick_any, face_pick), (facing_any, face_pair),
    )
    small = start_all(copies_of(small, small_sem))
    sends = []
    for part in range(parts):
        wait_all(large[part])
        build_table(verts, stiffness, table, part * rows, (part + 1) * rows)
    wait_all(small)

    @pl.loop(0, near.shape[0] // 8, unroll=16)
    def pairs(n):
        own, far = entry_at(table, local_pairs[0, 0, n]), entry_at(table, local_pairs[0, 1, n])
        near[pl.ds(pl.multiple_of(n * 8, 8), 8), :] = jnp.where(row < 4, own, far)

    sends += start_all(copies_of([(near, near_any)], out_sem, 4))

    @pl.loop(0, border.shape[0] // 8, unroll=16)
    def borders(n):
        border[pl.ds(pl.multiple_of(n * 8, 8), 8), :] = entry_at(table, border_pick[0, n])

    sends += start_all(copies_of([(border, border_out)], out_sem, 3))
    @pl.loop(0, face_lo.shape[0] // 8, unroll=8)
    def face(k):
        for side, out in ((0, face_lo), (1, face_hi)):
            target = face_pair[0, side, k]
            level = jnp.where(target >= 0, 0.0, OFF)
            own = entry_at(table, jnp.maximum(target, 0)) + jnp.where(row == 3, level, 0.0)
            out[pl.ds(pl.multiple_of(k * 8, 8), 8), :] = jnp.where(row < 4, own, entry_at(table, face_pick[0, side, k]))

    sends += start_all(copies_of([(face_lo, lo_any), (face_hi, hi_any)], out_sem, 1))

    bricks, slots = recv_pair.shape[1], recv_pair.shape[2]

    @pl.loop(0, bricks, unroll=2)
    def brick(s):
        for k in range(slots):
            target = recv_pair[0, s, k]
            wanted = jnp.where(target >= 0, recv_src[0, s, k], -1).astype(F32)
            entry = entry_at(table, jnp.maximum(target, 0))
            brick_msg[s * slots + k] = jnp.where(row == 3, wanted, entry)[0:4]

    sends += start_all(copies_of([(brick_msg, brick_any)], out_sem))

    wait_all(sends)


def write_planes(force, planes, planes_out, sem, before=None):
    parts = sem.shape[0]
    rows = planes.shape[1] // parts
    sends = []
    for part in range(parts):

        @pl.loop(part * rows // 8, (part + 1) * rows // 8, unroll=32)
        def unpack(n):
            here = pl.ds(pl.multiple_of(n * 8, 8), 8)
            for c in range(3):
                value = force[pl.ds(n * 64 + c, 8, stride=8), :]
                planes[c, here, :] = value if before is None else planes[c, here, :] + value

        here = pl.ds(part * rows, rows)
        sends += start_all([pltpu.make_async_copy(planes.at[:, here, :], planes_out.at[:, here, :], sem.at[part])])
    wait_all(sends)


def local_kernel(local_any, near_any, planes_out, local_pairs, near, force, planes, sem, plane_sem, *scratch):
    row = row_index()
    copies = start_all(copies_of([(local_any, local_pairs), (near_any, near)], sem))
    clear_rows(force)
    wait_all(copies)

    def load(n):
        entry = entry_at(near, n)
        own, far = split3(own_block(entry, row)), split3(far_block(entry, row))
        return (far, own), (own, far)

    def finish(n, push, react):
        entry = entry_at(near, n)
        add_at(force, local_pairs[0, 0, n], push_of(entry, push))
        add_at(force, local_pairs[0, 1, n], react_of(pltpu.roll(entry, 4, 0), react))

    pairs = local_pairs.shape[2]
    run_tiles(0, pairs, width_for(pairs), load, finish, scratch)
    write_planes(force, planes, planes_out, plane_sem)


def brick_kernel(border_any, message_any, after_any, back_any, react_any, border, message, back, react_out, index, sem, *scratch):
    row = row_index()
    count = message.shape[0]
    copies = [message_index(message_any, index, sem.at[2])]
    copies += copies_of(((border_any, border), (message_any, message)), sem)
    wait_all(start_all(copies))

    def far_entry(n):
        return entry_at(border, jnp.maximum(index[n, 0].astype(jnp.int32), 0))

    def load(n):
        x = jnp.concatenate([message[n], message[n]], axis=0)
        square = jnp.where(row < 3, x * x, 0.0)
        level = -0.5 * jnp.sum(square, axis=0, keepdims=True) + jnp.where(index[n, 0] >= 0.0, 0.0, OFF)
        own = split3(jnp.where(row == 3, level, jnp.where(row == 7, 1.0, x)))
        far = split3(far_block(far_entry(n), row))
        return (far, own), (own, far)

    def finish(n, push, react):
        back[n] = push_of(message[n], push[0:4])
        far = pltpu.roll(far_entry(n), 4, 0)
        react_out[pl.ds(pl.multiple_of(n * 8, 8), 8), :] = react_of(far, react)

    run_tiles(0, count, width_for(count), load, finish, scratch)
    copies = [
        pltpu.make_async_copy(back, back_any, sem.at[0]),
        pltpu.make_async_copy(react_out, react_any, sem.at[1]),
    ]
    for copy in copies:
        copy.start()
    for copy in copies:
        copy.wait()


def face_kernel(
    border_any, pick_any, pair_any, message, react_any, planes_in, sent_lo, sent_hi, got_lo, got_hi,
    planes_out, border_pick, face_pick, face_pair, brick_react, planes, force, sent, got, index, sem, plane_sem,
    *scratch,
):
    row = row_index()
    facing = face_pick.shape[2]
    copies = [message_index(message, index, sem.at[9])]
    for side, (mine, theirs) in enumerate(((sent_lo, got_lo), (sent_hi, got_hi))):
        here = pl.ds(side * facing * 8, facing * 8)
        copies.append(pltpu.make_async_copy(mine, sent.at[here], sem.at[side]))
        copies.append(pltpu.make_async_copy(theirs, got.at[here], sem.at[side + 2]))
    for n, (source, target) in enumerate(
        ((border_any, border_pick), (pick_any, face_pick), (pair_any, face_pair), (react_any, brick_react))
    ):
        copies.append(pltpu.make_async_copy(source, target, sem.at[n + 4]))
    before = pltpu.make_async_copy(planes_in, planes, sem.at[8])
    for copy in copies + [before]:
        copy.start()
    clear_rows(force)
    for copy in copies:
        copy.wait()

    @pl.loop(0, index.shape[0], unroll=8)
    def add_bricks(n):
        anchor = border_pick[0, jnp.maximum(index[n, 0].astype(jnp.int32), 0)]
        add_at(force, anchor, entry_at(brick_react, n))

    layer = lax.axis_index("slab")
    has_low, has_high = layer > 0, layer < lax.axis_size("slab") - 1

    def load(n):
        mine, theirs = entry_at(sent, n), entry_at(got, n)
        down = split3(far_block(theirs, row)), split3(own_block(theirs, row))
        return down, (split3(own_block(mine, row)), split3(far_block(mine, row)))

    def finish(n, push, react):
        side = (n >= facing).astype(jnp.int32)
        k = n - side * facing
        mine = entry_at(sent, n)
        add_at(force, jnp.maximum(face_pair[0, side, k], 0), push_of(mine, push))
        add_at(force, face_pick[0, side, k], react_of(pltpu.roll(mine, 4, 0), react))

    start = jnp.where(has_low, 0, facing)
    stop = jnp.where(has_high, 2 * facing, facing)
    run_tiles(start, stop, width_for(facing), load, finish, scratch)

    before.wait()
    write_planes(force, planes, planes_out, plane_sem, before)


def final_kernel(pair_any, planes_any, push_any, out_any, recv_pair, low, mid, high, brick_push, in_sem, out_sem):
    planes = (low, mid, high)
    small = start_all(copies_of(((push_any, brick_push), (pair_any, recv_pair)), in_sem, 3))
    large = start_all(copies_of([(planes_any.at[c], plane) for c, plane in enumerate(planes)], in_sem))
    bricks, slots = recv_pair.shape[1], recv_pair.shape[2]
    wait_all(small)
    sends = []
    for c, plane in enumerate(planes):
        large[c].wait()

        @pl.loop(0, bricks)
        def brick(s):
            for k in range(slots):
                target = recv_pair[0, s, k]
                push = jnp.where(target >= 0, brick_push[s * slots + k, c:c + 1], 0.0)
                plane[pl.ds(jnp.maximum(target, 0), 1), :] += push

        sends += start_all(copies_of([(plane, out_any.at[c])], out_sem, c))
    wait_all(sends)


HBM = pl.BlockSpec(memory_space=pltpu.HBM)


def call(kernel, out, in_specs, out_specs, scratch, cost):
    return pl.pallas_call(
        kernel,
        out_shape=out,
        in_specs=in_specs,
        out_specs=out_specs,
        scratch_shapes=scratch,
        compiler_params=pltpu.CompilerParams(vmem_limit_bytes=VMEM_LIMIT),
        cost_estimate=pl.CostEstimate(flops=cost[0], bytes_accessed=cost[1], transcendentals=cost[2]),
    )


def shape(*dims):
    return jax.ShapeDtypeStruct(dims, F32)


def body(verts, stiffness, local_pairs, border_pick, recv_src, recv_pair, face_pick, face_pair):
    patches = verts.shape[0]
    bricks, slots = recv_pair.shape[1], recv_pair.shape[2]
    facing = face_pick.shape[2]
    count = bricks * slots
    pairs = local_pairs.shape[2]
    layers = lax.axis_size("slab")
    tile = 128 * 128

    near, brick_msg, face_lo, face_hi, border = call(
        pack_kernel,
        (
            shape(pairs * 8, 128), shape(count, 4, 128), shape(facing * 8, 128), shape(facing * 8, 128),
            shape(border_pick.shape[1] * 8, 128),
        ),
        [HBM] * 8,
        (HBM,) * 5,
        scratch=[pltpu.SMEM(array.shape, jnp.int32) for array in (local_pairs, border_pick, recv_src, recv_pair, face_pick, face_pair)]
        + [
            pltpu.VMEM((3, patches, 128), F32),
            pltpu.VMEM((patches, 128), F32),
            pltpu.VMEM((patches * 8, 128), F32),
            pltpu.VMEM((pairs * 8, 128), F32),
            pltpu.VMEM((count, 4, 128), F32),
            pltpu.VMEM((facing * 8, 128), F32),
            pltpu.VMEM((facing * 8, 128), F32),
            pltpu.VMEM((border_pick.shape[1] * 8, 128), F32),
        ]
        + [pltpu.SemaphoreType.DMA((n,)) for n in (6, 8, 5)],
        cost=(patches * 128 * 60, patches * 128 * 48, 0),
    )(
        local_pairs, border_pick, recv_src, recv_pair, face_pick, face_pair,
        jnp.transpose(verts, (1, 0, 2)), stiffness,
    )

    arrived = lax.all_to_all(brick_msg, "brick", 0, 0, tiled=True)
    got_hi = lax.ppermute(face_lo, "slab", [((i + 1) % layers, i) for i in range(layers)])
    got_lo = lax.ppermute(face_hi, "slab", [(i, (i + 1) % layers) for i in range(layers)])

    planes = call(
        local_kernel,
        shape(3, patches, 128),
        [HBM] * 2,
        HBM,
        scratch=[
            pltpu.SMEM(local_pairs.shape, jnp.int32),
            pltpu.VMEM((pairs * 8, 128), F32),
            pltpu.VMEM((patches * 8, 128), F32),
            pltpu.VMEM((3, patches, 128), F32),
            pltpu.SemaphoreType.DMA((2,)),
            pltpu.SemaphoreType.DMA((4,)),
        ]
        + tile_scratch(WIDTH),
        cost=(pairs * tile * 400, patches * 128 * 48, pairs * tile),
    )(local_pairs, near)

    back, brick_react = call(
        brick_kernel,
        (shape(count, 4, 128), shape(count * 8, 128)),
        [HBM, HBM, HBM],
        (HBM, HBM),
        scratch=[
            pltpu.VMEM(border.shape, F32),
            pltpu.VMEM(arrived.shape, F32),
            pltpu.VMEM((count, 4, 128), F32),
            pltpu.VMEM((count * 8, 128), F32),
            pltpu.SMEM((count, 128), F32),
            pltpu.SemaphoreType.DMA((3,)),
        ]
        + tile_scratch(WIDTH),
        cost=(count * tile * 400, patches * 128 * 32, count * tile),
    )(border, arrived, planes)

    brick_push = lax.all_to_all(back, "brick", 0, 0, tiled=True)
    planes = call(
        face_kernel,
        shape(3, patches, 128),
        [HBM] * 10,
        HBM,
        scratch=[
            pltpu.SMEM(border_pick.shape, jnp.int32),
            pltpu.SMEM(face_pick.shape, jnp.int32),
            pltpu.SMEM(face_pair.shape, jnp.int32),
            pltpu.VMEM((count * 8, 128), F32),
            pltpu.VMEM((3, patches, 128), F32),
            pltpu.VMEM((patches * 8, 128), F32),
            pltpu.VMEM((2 * facing * 8, 128), F32),
            pltpu.VMEM((2 * facing * 8, 128), F32),
            pltpu.SMEM((count, 128), F32),
            pltpu.SemaphoreType.DMA((10,)),
            pltpu.SemaphoreType.DMA((4,)),
        ]
        + tile_scratch(WIDTH),
        cost=(4 * facing * tile * 400, patches * 128 * 64, 4 * facing * tile),
    )(border_pick, face_pick, face_pair, arrived, brick_react, planes, face_lo, face_hi, got_lo, got_hi)

    out = call(
        final_kernel,
        shape(3, patches, 128),
        [HBM, HBM, HBM],
        HBM,
        scratch=[pltpu.SMEM(recv_pair.shape, jnp.int32)]
        + [pltpu.VMEM((patches, 128), F32)] * 3
        + [pltpu.VMEM((count, 4, 128), F32), pltpu.SemaphoreType.DMA((5,)), pltpu.SemaphoreType.DMA((3,))],
        cost=(count * 128 * 24, patches * 128 * 24, 0),
    )(recv_pair, planes, brick_push)
    return jnp.transpose(out, (1, 0, 2))


def solution(mesh):
    placed = (
        P(("slab", "brick"), None, None),
        P(("slab", "brick"), None),
        P(("slab", "brick"), None, None),
        P(("slab", "brick"), None),
        P(("slab", "brick"), None, None),
        P(("slab", "brick"), None, None),
        P(("slab", "brick"), None, None),
        P(("slab", "brick"), None, None),
    )
    return jax.shard_map(
        body,
        mesh=mesh,
        in_specs=placed,
        out_specs=P(("slab", "brick"), None, None),
        check_vma=False,
    )
```

```python
import math

import jax
import jax.numpy as jnp
from jax import lax
from jax.experimental import pallas as pl
from jax.experimental.pallas import tpu as pltpu
from jax.sharding import PartitionSpec as P

F32 = jnp.float32
BF16 = jnp.bfloat16
ALPHA = math.sqrt(math.log2(math.e))
PUSH = 1.0 / ALPHA
REACT = 1.0 / (3.0 * ALPHA)
OFF = -1.0e5
VMEM_LIMIT = 64 * 1024 * 1024
WIDTH = 8
MATMUL = (((1,), (0,)), ((), ()))


def row_index():
    return lax.broadcasted_iota(jnp.int32, (8, 128), 0)


def split3(x):
    high = x.astype(BF16).astype(F32)
    rest = x - high
    mid = rest.astype(BF16).astype(F32)
    return high, mid, rest - mid


def own_block(entry, row):
    return jnp.where(row < 4, entry, jnp.where(row == 7, 1.0, pltpu.roll(entry, 4, 0)))


def far_block(entry, row):
    return jnp.where(row < 3, pltpu.roll(entry, 4, 0), jnp.where(row == 3, 1.0, entry))


def own_rows(parts, row):
    high, mid, low = parts
    one = jnp.where(row == 7, 1.0, 0.0)
    return [high, mid + one, jnp.where(row < 3, high, low) + one]


def far_rows(parts, row):
    high, mid, low = parts
    copy = (row >= 4) & (row < 7)
    return [
        jnp.where(copy, mid, high),
        jnp.where(row < 4, high, mid),
        jnp.where((row >= 3) & (row < 7), high, low),
    ]


def entry_at(ref, index):
    return ref[pl.ds(pl.multiple_of(index * 8, 8), 8), :]


def add_at(ref, index, value):
    ref[pl.ds(pl.multiple_of(index * 8, 8), 8), :] += value


def spread(react):
    return react + pltpu.roll(react, 1, 1) + pltpu.roll(react, 2, 1)


def tile_scratch(width):
    return [
        pltpu.VMEM((2 * width, 128, 48), BF16),
        pltpu.VMEM((2 * width, 48, 256), BF16),
        pltpu.VMEM((2 * width, 32, 128), BF16),
        pltpu.VMEM((2 * width, 128, 256), BF16),
        pltpu.VMEM((2 * width, 128, 256), BF16),
        pltpu.VMEM((2 * width, 2, 8, 128), F32),
    ]


def run_tiles(start, stop, width, load, finish, scratch, filled=None, beside=None):
    lefts, rights, thins, highs, lows, sums = scratch
    row = row_index()

    def prepare(n, slot):
        (far_down, own_down), (own_across, far_across) = load(n)
        left = far_rows(far_down, row) + own_rows(own_down, row)
        empty = [jnp.zeros((8, 128), F32)] * 3
        first = jnp.concatenate(own_rows(own_across, row) + empty, axis=0)
        second = jnp.concatenate(empty + far_rows(far_across, row), axis=0)
        lefts[slot] = jnp.concatenate(left, axis=0).astype(BF16).T
        rights[slot] = jnp.concatenate([first, second], axis=1).astype(BF16)
        thin = jnp.concatenate([far_down[0], far_down[1], own_down[0], own_down[1]], axis=0)
        thins[slot] = thin.astype(BF16)

    def energies(slot):
        energy = jnp.exp2(lax.dot_general(lefts[slot], rights[slot], MATMUL, preferred_element_type=F32))
        high = energy.astype(BF16)
        highs[slot] = high
        lows[slot] = (energy - high.astype(F32)).astype(BF16)

    def totals(slot):
        tall = jnp.concatenate([highs[slot], lows[slot]], axis=0)
        thin = jnp.concatenate([thins[slot], thins[slot]], axis=1)
        result = lax.dot_general(thin, tall, MATMUL, preferred_element_type=F32)
        push = result[0:8, 0:128] + result[8:16, 0:128]
        react = result[16:24, 128:256] + result[24:32, 128:256]
        return push, react

    last = stop - 1
    for q in range(2 * width):
        prepare(jnp.minimum(start + q, last), q)
    for q in range(width):
        energies(q)

    sums[width : 2 * width] = jnp.zeros((width, 2, 8, 128), F32)
    if filled is not None:
        filled()

    @pl.loop(0, (stop - start) // (2 * width))
    def step(m):
        base = start + m * (2 * width)
        for half in range(2):
            here, there = half * width, (1 - half) * width
            for q in range(width):
                finish(jnp.maximum(base + here + q - width, start), sums[there + q, 0], sums[there + q, 1])
                if beside is not None:
                    beside(base + here + q)
                sums[here + q, 0], sums[here + q, 1] = totals(here + q)
                energies(there + q)
                prepare(jnp.minimum(base + 2 * width + here + q, last), here + q)

    for q in range(width):
        finish(stop - width + q, sums[width + q, 0], sums[width + q, 1])


def push_of(own, total):
    return (own * total[3:4] - total) * PUSH


def react_of(far, total):
    return spread((far * total[7:8] - total) * REACT)


def width_for(couples):
    return max(width for width in range(1, WIDTH + 1) if couples % (2 * width) == 0)


def build_table(verts, stiffness, table, first, last):
    @pl.loop(first // 8, last // 8, unroll=32)
    def build(step):
        base = pl.multiple_of(step * 8, 8)
        xs = [verts[c, pl.ds(base, 8), :] * ALPHA for c in range(3)]
        cs = [(x + pltpu.roll(x, 127, 1) + pltpu.roll(x, 126, 1)) * (1.0 / 3.0) for x in xs]
        strength = stiffness[pl.ds(base, 8), :]
        own = -0.5 * (xs[0] * xs[0] + xs[1] * xs[1] + xs[2] * xs[2])
        far = jnp.log2(strength) - 7.0 - 0.5 * (cs[0] * cs[0] + cs[1] * cs[1] + cs[2] * cs[2])
        for k, value in enumerate(xs + [own] + cs + [far]):
            table[pl.ds(step * 64 + k, 8, stride=8), :] = value


def clear_rows(ref):
    @pl.loop(0, ref.shape[0] // 64, unroll=8)
    def clear(n):
        ref[pl.ds(pl.multiple_of(n * 64, 64), 64), :] = jnp.zeros((64, 128), F32)


def slot_of(n, slots):
    return n + jnp.where(n >= lax.axis_index("brick") * slots, slots, 0)


def message_index(message, index, sem):
    return pltpu.make_async_copy(message.at[:, 3, :], index, sem)


def start_all(copies):
    for copy in copies:
        copy.start()
    return copies


def wait_all(copies):
    for copy in copies:
        copy.wait()


def copies_of(pairs, sem, first=0):
    return [pltpu.make_async_copy(source, target, sem.at[first + n]) for n, (source, target) in enumerate(pairs)]


def ask_kernel(src_any, pair_any, verts_any, brick_any, recv_src, recv_pair, verts, brick_msg, sem):
    wait_all(start_all(copies_of(((src_any, recv_src), (pair_any, recv_pair), (verts_any, verts)), sem)))
    bricks, slots = recv_pair.shape[1], recv_pair.shape[2]

    @pl.loop(0, bricks, unroll=4)
    def brick(s):
        for k in range(slots):
            target = recv_pair[0, s, k]
            wanted = jnp.where(target >= 0, recv_src[0, s, k], -1).astype(F32)
            place = pl.ds(jnp.maximum(target, 0), 1)
            for c in range(3):
                brick_msg[s * slots + k, c:c + 1] = verts[c, place, :] * ALPHA
            brick_msg[s * slots + k, 3:4] = jnp.full((1, 128), wanted, F32)

    wait_all(start_all(copies_of([(brick_msg, brick_any)], sem)))


def pack_kernel(
    local_any, border_any, pick_any, facing_any, verts_any, stiffness_any,
    near_any, lo_any, hi_any, border_out,
    local_pairs, border_pick, face_pick, face_pair, verts, stiffness, table, near,
    face_lo, face_hi, border, small_sem, large_sem, out_sem,
):
    patches = stiffness.shape[0]
    row = row_index()
    parts = large_sem.shape[0] // 2
    rows = patches // parts
    large = []
    for part in range(parts):
        here = pl.ds(part * rows, rows)
        pieces = ((verts_any.at[:, here, :], verts.at[:, here, :]), (stiffness_any.at[here], stiffness.at[here]))
        large.append(start_all(copies_of(pieces, large_sem, 2 * part)))
    small = (
        (local_any, local_pairs), (border_any, border_pick), (pick_any, face_pick), (facing_any, face_pair),
    )
    small = start_all(copies_of(small, small_sem))
    sends = []
    for part in range(parts):
        wait_all(large[part])
        build_table(verts, stiffness, table, part * rows, (part + 1) * rows)
    wait_all(small)

    @pl.loop(0, near.shape[0] // 8, unroll=16)
    def pairs(n):
        own, far = entry_at(table, local_pairs[0, 0, n]), entry_at(table, local_pairs[0, 1, n])
        near[pl.ds(pl.multiple_of(n * 8, 8), 8), :] = jnp.where(row < 4, own, far)

    sends += start_all(copies_of([(near, near_any)], out_sem))

    @pl.loop(0, border.shape[0] // 8, unroll=16)
    def borders(n):
        border[pl.ds(pl.multiple_of(n * 8, 8), 8), :] = entry_at(table, border_pick[0, n])

    sends += start_all(copies_of([(border, border_out)], out_sem, 3))
    @pl.loop(0, face_lo.shape[0] // 8, unroll=8)
    def face(k):
        for side, out in ((0, face_lo), (1, face_hi)):
            target = face_pair[0, side, k]
            level = jnp.where(target >= 0, 0.0, OFF)
            own = entry_at(table, jnp.maximum(target, 0)) + jnp.where(row == 3, level, 0.0)
            out[pl.ds(pl.multiple_of(k * 8, 8), 8), :] = jnp.where(row < 4, own, entry_at(table, face_pick[0, side, k]))

    sends += start_all(copies_of([(face_lo, lo_any), (face_hi, hi_any)], out_sem, 1))

    wait_all(sends)


def write_planes(force, planes, planes_out, sem, before=None):
    parts = sem.shape[0]
    rows = planes.shape[1] // parts
    sends = []
    for part in range(parts):

        @pl.loop(part * rows // 8, (part + 1) * rows // 8, unroll=32)
        def unpack(n):
            here = pl.ds(pl.multiple_of(n * 8, 8), 8)
            for c in range(3):
                value = force[pl.ds(n * 64 + c, 8, stride=8), :]
                planes[c, here, :] = value if before is None else planes[c, here, :] + value

        here = pl.ds(part * rows, rows)
        sends += start_all([pltpu.make_async_copy(planes.at[:, here, :], planes_out.at[:, here, :], sem.at[part])])
    wait_all(sends)


def local_kernel(local_any, near_any, after_any, planes_out, local_pairs, near, force, planes, sem, plane_sem, *scratch):
    row = row_index()
    pairs = local_pairs.shape[2]
    width = width_for(pairs)
    first = pl.ds(0, 2 * width * 8)
    rest = pl.ds(2 * width * 8, (pairs - 2 * width) * 8)
    copies = start_all(copies_of([(near_any.at[first], near.at[first])], sem))
    others = start_all(copies_of([(local_any, local_pairs), (near_any.at[rest], near.at[rest])], sem, 1))
    clear_rows(force)
    wait_all(copies)

    def load(n):
        entry = entry_at(near, n)
        own, far = split3(own_block(entry, row)), split3(far_block(entry, row))
        return (far, own), (own, far)

    def finish(n, push, react):
        entry = entry_at(near, n)
        add_at(force, local_pairs[0, 0, n], push_of(entry, push))
        add_at(force, local_pairs[0, 1, n], react_of(pltpu.roll(entry, 4, 0), react))

    run_tiles(0, pairs, width, load, finish, scratch, lambda: wait_all(others))
    write_planes(force, planes, planes_out, plane_sem)


def brick_kernel(border_any, message_any, back_any, react_any, border, message, back, react_out, index, sem, *scratch):
    row = row_index()
    count = message.shape[0]
    copies = [message_index(message_any, index, sem.at[2])]
    copies += copies_of(((border_any, border), (message_any, message)), sem)
    wait_all(start_all(copies))

    slots = count // lax.axis_size("brick")

    def far_entry(n):
        return entry_at(border, jnp.maximum(index[n, 0].astype(jnp.int32), 0))

    def load(n):
        n = slot_of(n, slots)
        x = jnp.concatenate([message[n], message[n]], axis=0)
        square = jnp.where(row < 3, x * x, 0.0)
        level = -0.5 * jnp.sum(square, axis=0, keepdims=True) + jnp.where(index[n, 0] >= 0.0, 0.0, OFF)
        own = split3(jnp.where(row == 3, level, jnp.where(row == 7, 1.0, x)))
        far = split3(far_block(far_entry(n), row))
        return (far, own), (own, far)

    def finish(n, push, react):
        n = slot_of(n, slots)
        back[n] = push_of(message[n], push[0:4])
        far = pltpu.roll(far_entry(n), 4, 0)
        react_out[pl.ds(pl.multiple_of(n * 8, 8), 8), :] = react_of(far, react)

    couples = count - slots
    run_tiles(0, couples, width_for(couples), load, finish, scratch)
    copies = [
        pltpu.make_async_copy(back, back_any, sem.at[0]),
        pltpu.make_async_copy(react_out, react_any, sem.at[1]),
    ]
    for copy in copies:
        copy.start()
    for copy in copies:
        copy.wait()


def face_kernel(
    border_any, pick_any, pair_any, asked_any, message, react_any, push_any, planes_in, sent_lo, sent_hi, got_lo, got_hi,
    planes_out, border_pick, face_pick, face_pair, recv_pair, brick_react, brick_push, planes, force, sent, got, index, sem, plane_sem,
    *scratch,
):
    row = row_index()
    facing = face_pick.shape[2]
    copies = [message_index(message, index, sem.at[11])]
    for side, (mine, theirs) in enumerate(((sent_lo, got_lo), (sent_hi, got_hi))):
        here = pl.ds(side * facing * 8, facing * 8)
        copies.append(pltpu.make_async_copy(mine, sent.at[here], sem.at[side]))
        copies.append(pltpu.make_async_copy(theirs, got.at[here], sem.at[side + 2]))
    for n, (source, target) in enumerate(
        (
            (border_any, border_pick), (pick_any, face_pick), (pair_any, face_pair), (react_any, brick_react),
            (asked_any, recv_pair), (push_any, brick_push),
        )
    ):
        copies.append(pltpu.make_async_copy(source, target, sem.at[n + 4]))
    before = pltpu.make_async_copy(planes_in, planes, sem.at[10])
    for copy in copies + [before]:
        copy.start()
    clear_rows(force)
    for copy in copies:
        copy.wait()

    layer = lax.axis_index("slab")
    has_low, has_high = layer > 0, layer < lax.axis_size("slab") - 1

    start = jnp.where(has_low, 0, facing)
    stop = jnp.where(has_high, 2 * facing, facing)
    bricks, slots = recv_pair.shape[1], recv_pair.shape[2]

    @pl.loop(0, bricks - 1, unroll=1)
    def add_bricks(n):
        s = n + jnp.where(n >= lax.axis_index("brick"), 1, 0)
        for k in range(slots):
            slot = s * slots + k
            anchor = border_pick[0, jnp.maximum(index[slot, 0].astype(jnp.int32), 0)]
            add_at(force, anchor, entry_at(brick_react, slot))
            target = recv_pair[0, s, k]
            push = jnp.concatenate([brick_push[slot], jnp.zeros((4, 128), F32)], axis=0)
            add_at(force, jnp.maximum(target, 0), jnp.where(target >= 0, push, 0.0))

    def load(n):
        mine, theirs = entry_at(sent, n), entry_at(got, n)
        down = split3(far_block(theirs, row)), split3(own_block(theirs, row))
        return down, (split3(own_block(mine, row)), split3(far_block(mine, row)))

    def finish(n, push, react):
        side = (n >= facing).astype(jnp.int32)
        k = n - side * facing
        mine = entry_at(sent, n)
        add_at(force, jnp.maximum(face_pair[0, side, k], 0), push_of(mine, push))
        add_at(force, face_pick[0, side, k], react_of(pltpu.roll(mine, 4, 0), react))

    run_tiles(start, stop, width_for(facing), load, finish, scratch)

    before.wait()
    write_planes(force, planes, planes_out, plane_sem, before)


HBM = pl.BlockSpec(memory_space=pltpu.HBM)


def call(kernel, out, in_specs, out_specs, scratch, cost):
    return pl.pallas_call(
        kernel,
        out_shape=out,
        in_specs=in_specs,
        out_specs=out_specs,
        scratch_shapes=scratch,
        compiler_params=pltpu.CompilerParams(vmem_limit_bytes=VMEM_LIMIT),
        cost_estimate=pl.CostEstimate(flops=cost[0], bytes_accessed=cost[1], transcendentals=cost[2]),
    )


def shape(*dims):
    return jax.ShapeDtypeStruct(dims, F32)


def body(verts, stiffness, local_pairs, border_pick, recv_src, recv_pair, face_pick, face_pair):
    patches = verts.shape[0]
    bricks, slots = recv_pair.shape[1], recv_pair.shape[2]
    facing = face_pick.shape[2]
    count = bricks * slots
    pairs = local_pairs.shape[2]
    layers = lax.axis_size("slab")
    tile = 128 * 128

    points = jnp.transpose(verts, (1, 0, 2))
    brick_msg = call(
        ask_kernel,
        shape(count, 4, 128),
        [HBM] * 3,
        HBM,
        scratch=[
            pltpu.SMEM(recv_src.shape, jnp.int32),
            pltpu.SMEM(recv_pair.shape, jnp.int32),
            pltpu.VMEM((3, patches, 128), F32),
            pltpu.VMEM((count, 4, 128), F32),
            pltpu.SemaphoreType.DMA((3,)),
        ],
        cost=(count * 512, patches * 128 * 12, 0),
    )(recv_src, recv_pair, points)
    arrived = lax.all_to_all(brick_msg, "brick", 0, 0, tiled=True)

    near, face_lo, face_hi, border = call(
        pack_kernel,
        (
            shape(pairs * 8, 128), shape(facing * 8, 128), shape(facing * 8, 128),
            shape(border_pick.shape[1] * 8, 128),
        ),
        [HBM] * 6,
        (HBM,) * 4,
        scratch=[pltpu.SMEM(array.shape, jnp.int32) for array in (local_pairs, border_pick, face_pick, face_pair)]
        + [
            pltpu.VMEM((3, patches, 128), F32),
            pltpu.VMEM((patches, 128), F32),
            pltpu.VMEM((patches * 8, 128), F32),
            pltpu.VMEM((pairs * 8, 128), F32),
            pltpu.VMEM((facing * 8, 128), F32),
            pltpu.VMEM((facing * 8, 128), F32),
            pltpu.VMEM((border_pick.shape[1] * 8, 128), F32),
        ]
        + [pltpu.SemaphoreType.DMA((n,)) for n in (4, 8, 4)],
        cost=(patches * 128 * 60, patches * 128 * 48, 0),
    )(local_pairs, border_pick, face_pick, face_pair, points, stiffness)

    got_hi = lax.ppermute(face_lo, "slab", [((i + 1) % layers, i) for i in range(layers)])
    got_lo = lax.ppermute(face_hi, "slab", [(i, (i + 1) % layers) for i in range(layers)])

    back, brick_react = call(
        brick_kernel,
        (shape(count, 4, 128), shape(count * 8, 128)),
        [HBM, HBM],
        (HBM, HBM),
        scratch=[
            pltpu.VMEM(border.shape, F32),
            pltpu.VMEM(arrived.shape, F32),
            pltpu.VMEM((count, 4, 128), F32),
            pltpu.VMEM((count * 8, 128), F32),
            pltpu.SMEM((count, 128), F32),
            pltpu.SemaphoreType.DMA((3,)),
        ]
        + tile_scratch(WIDTH),
        cost=(count * tile * 400, patches * 128 * 32, count * tile),
    )(border, arrived)

    brick_push = lax.all_to_all(back, "brick", 0, 0, tiled=True)
    planes = call(
        local_kernel,
        shape(3, patches, 128),
        [HBM] * 3,
        HBM,
        scratch=[
            pltpu.SMEM(local_pairs.shape, jnp.int32),
            pltpu.VMEM((pairs * 8, 128), F32),
            pltpu.VMEM((patches * 8, 128), F32),
            pltpu.VMEM((3, patches, 128), F32),
            pltpu.SemaphoreType.DMA((3,)),
            pltpu.SemaphoreType.DMA((4,)),
        ]
        + tile_scratch(WIDTH),
        cost=(pairs * tile * 400, patches * 128 * 48, pairs * tile),
    )(local_pairs, near, back)

    out = call(
        face_kernel,
        shape(3, patches, 128),
        [HBM] * 12,
        HBM,
        scratch=[
            pltpu.SMEM(border_pick.shape, jnp.int32),
            pltpu.SMEM(face_pick.shape, jnp.int32),
            pltpu.SMEM(face_pair.shape, jnp.int32),
            pltpu.SMEM(recv_pair.shape, jnp.int32),
            pltpu.VMEM((count * 8, 128), F32),
            pltpu.VMEM((count, 4, 128), F32),
            pltpu.VMEM((3, patches, 128), F32),
            pltpu.VMEM((patches * 8, 128), F32),
            pltpu.VMEM((2 * facing * 8, 128), F32),
            pltpu.VMEM((2 * facing * 8, 128), F32),
            pltpu.SMEM((count, 128), F32),
            pltpu.SemaphoreType.DMA((12,)),
            pltpu.SemaphoreType.DMA((4,)),
        ]
        + tile_scratch(WIDTH),
        cost=(4 * facing * tile * 400, patches * 128 * 64, 4 * facing * tile),
    )(
        border_pick, face_pick, face_pair, recv_pair, arrived, brick_react, brick_push, planes,
        face_lo, face_hi, got_lo, got_hi,
    )
    return jnp.transpose(out, (1, 0, 2))


def solution(mesh):
    placed = (
        P(("slab", "brick"), None, None),
        P(("slab", "brick"), None),
        P(("slab", "brick"), None, None),
        P(("slab", "brick"), None),
        P(("slab", "brick"), None, None),
        P(("slab", "brick"), None, None),
        P(("slab", "brick"), None, None),
        P(("slab", "brick"), None, None),
    )
    return jax.shard_map(
        body,
        mesh=mesh,
        in_specs=placed,
        out_specs=P(("slab", "brick"), None, None),
        check_vma=False,
    )
```

```python
import math

import jax
import jax.numpy as jnp
from jax import lax
from jax.experimental import pallas as pl
from jax.experimental.pallas import tpu as pltpu
from jax.sharding import PartitionSpec as P

F32 = jnp.float32
BF16 = jnp.bfloat16
ALPHA = math.sqrt(math.log2(math.e))
PUSH = 1.0 / ALPHA
REACT = 1.0 / (3.0 * ALPHA)
OFF = -1.0e5
VMEM_LIMIT = 64 * 1024 * 1024
WIDTH = 8
MATMUL = (((1,), (0,)), ((), ()))


def row_index():
    return lax.broadcasted_iota(jnp.int32, (8, 128), 0)


def split3(x):
    high = x.astype(BF16).astype(F32)
    rest = x - high
    mid = rest.astype(BF16).astype(F32)
    return high, mid, rest - mid


def own_block(entry, row):
    return jnp.where(row < 4, entry, jnp.where(row == 7, 1.0, pltpu.roll(entry, 4, 0)))


def far_block(entry, row):
    return jnp.where(row < 3, pltpu.roll(entry, 4, 0), jnp.where(row == 3, 1.0, entry))


def own_rows(parts, row):
    high, mid, low = parts
    one = jnp.where(row == 7, 1.0, 0.0)
    return [high, mid + one, jnp.where(row < 3, high, low) + one]


def far_rows(parts, row):
    high, mid, low = parts
    copy = (row >= 4) & (row < 7)
    return [
        jnp.where(copy, mid, high),
        jnp.where(row < 4, high, mid),
        jnp.where((row >= 3) & (row < 7), high, low),
    ]


def entry_at(ref, index):
    return ref[pl.ds(pl.multiple_of(index * 8, 8), 8), :]


def add_at(ref, index, value):
    ref[pl.ds(pl.multiple_of(index * 8, 8), 8), :] += value


def spread(react):
    return react + pltpu.roll(react, 1, 1) + pltpu.roll(react, 2, 1)


def tile_scratch(width):
    return [
        pltpu.VMEM((2 * width, 128, 48), BF16),
        pltpu.VMEM((2 * width, 48, 256), BF16),
        pltpu.VMEM((2 * width, 32, 128), BF16),
        pltpu.VMEM((2 * width, 128, 256), BF16),
        pltpu.VMEM((2 * width, 128, 256), BF16),
        pltpu.VMEM((2 * width, 2, 8, 128), F32),
    ]


def run_tiles(start, stop, width, load, finish, scratch, filled=None, beside=None):
    lefts, rights, thins, highs, lows, sums = scratch
    row = row_index()

    def prepare(n, slot):
        (far_down, own_down), (own_across, far_across) = load(n)
        left = far_rows(far_down, row) + own_rows(own_down, row)
        empty = [jnp.zeros((8, 128), F32)] * 3
        first = jnp.concatenate(own_rows(own_across, row) + empty, axis=0)
        second = jnp.concatenate(empty + far_rows(far_across, row), axis=0)
        lefts[slot] = jnp.concatenate(left, axis=0).astype(BF16).T
        rights[slot] = jnp.concatenate([first, second], axis=1).astype(BF16)
        thin = jnp.concatenate([far_down[0], far_down[1], own_down[0], own_down[1]], axis=0)
        thins[slot] = thin.astype(BF16)

    def energies(slot):
        energy = jnp.exp2(lax.dot_general(lefts[slot], rights[slot], MATMUL, preferred_element_type=F32))
        high = energy.astype(BF16)
        highs[slot] = high
        lows[slot] = (energy - high.astype(F32)).astype(BF16)

    def totals(slot):
        tall = jnp.concatenate([highs[slot], lows[slot]], axis=0)
        thin = jnp.concatenate([thins[slot], thins[slot]], axis=1)
        result = lax.dot_general(thin, tall, MATMUL, preferred_element_type=F32)
        push = result[0:8, 0:128] + result[8:16, 0:128]
        react = result[16:24, 128:256] + result[24:32, 128:256]
        return push, react

    last = stop - 1
    for q in range(2 * width):
        prepare(jnp.minimum(start + q, last), q)
    for q in range(width):
        energies(q)

    sums[width : 2 * width] = jnp.zeros((width, 2, 8, 128), F32)
    if filled is not None:
        filled()

    @pl.loop(0, (stop - start) // (2 * width))
    def step(m):
        base = start + m * (2 * width)
        for half in range(2):
            here, there = half * width, (1 - half) * width
            for q in range(width):
                finish(jnp.maximum(base + here + q - width, start), sums[there + q, 0], sums[there + q, 1])
                if beside is not None:
                    beside(base + here + q)
                sums[here + q, 0], sums[here + q, 1] = totals(here + q)
                energies(there + q)
                prepare(jnp.minimum(base + 2 * width + here + q, last), here + q)

    for q in range(width):
        finish(stop - width + q, sums[width + q, 0], sums[width + q, 1])


def push_of(own, total):
    return (own * total[3:4] - total) * PUSH


def react_of(far, total):
    return spread((far * total[7:8] - total) * REACT)


def width_for(couples):
    return max(width for width in range(1, WIDTH + 1) if couples % (2 * width) == 0)


def build_table(verts, stiffness, table, first, last):
    @pl.loop(first // 8, last // 8, unroll=32)
    def build(step):
        base = pl.multiple_of(step * 8, 8)
        xs = [verts[c, pl.ds(base, 8), :] * ALPHA for c in range(3)]
        cs = [(x + pltpu.roll(x, 127, 1) + pltpu.roll(x, 126, 1)) * (1.0 / 3.0) for x in xs]
        strength = stiffness[pl.ds(base, 8), :]
        own = -0.5 * (xs[0] * xs[0] + xs[1] * xs[1] + xs[2] * xs[2])
        far = jnp.log2(strength) - 7.0 - 0.5 * (cs[0] * cs[0] + cs[1] * cs[1] + cs[2] * cs[2])
        for k, value in enumerate(xs + [own] + cs + [far]):
            table[pl.ds(step * 64 + k, 8, stride=8), :] = value


def clear_rows(ref):
    @pl.loop(0, ref.shape[0] // 64, unroll=8)
    def clear(n):
        ref[pl.ds(pl.multiple_of(n * 64, 64), 64), :] = jnp.zeros((64, 128), F32)


def slot_of(n, slots):
    return n + jnp.where(n >= lax.axis_index("brick") * slots, slots, 0)


def message_index(message, index, sem):
    return pltpu.make_async_copy(message.at[:, 3, :], index, sem)


def start_all(copies):
    for copy in copies:
        copy.start()
    return copies


def wait_all(copies):
    for copy in copies:
        copy.wait()


def copies_of(pairs, sem, first=0):
    return [pltpu.make_async_copy(source, target, sem.at[first + n]) for n, (source, target) in enumerate(pairs)]


def ask_kernel(src_any, pair_any, verts_any, brick_any, recv_src, recv_pair, verts, brick_msg, sem):
    wait_all(start_all(copies_of(((src_any, recv_src), (pair_any, recv_pair), (verts_any, verts)), sem)))
    bricks, slots = recv_pair.shape[1], recv_pair.shape[2]

    @pl.loop(0, bricks, unroll=4)
    def brick(s):
        for k in range(slots):
            target = recv_pair[0, s, k]
            wanted = jnp.where(target >= 0, recv_src[0, s, k], -1).astype(F32)
            place = pl.ds(jnp.maximum(target, 0), 1)
            for c in range(3):
                brick_msg[s * slots + k, c:c + 1] = verts[c, place, :] * ALPHA
            brick_msg[s * slots + k, 3:4] = jnp.full((1, 128), wanted, F32)

    wait_all(start_all(copies_of([(brick_msg, brick_any)], sem)))


def pack_kernel(
    local_any, border_any, pick_any, facing_any, verts_any, stiffness_any,
    near_any, lo_any, hi_any, border_out,
    own_side, far_side, border_pick, face_pick, face_pair, verts, stiffness, table, near,
    face_lo, face_hi, border, small_sem, large_sem, out_sem,
):
    patches = stiffness.shape[0]
    row = row_index()
    parts = large_sem.shape[0] // 2
    rows = patches // parts
    large = []
    for part in range(parts):
        here = pl.ds(part * rows, rows)
        pieces = ((verts_any.at[:, here, :], verts.at[:, here, :]), (stiffness_any.at[here], stiffness.at[here]))
        large.append(start_all(copies_of(pieces, large_sem, 2 * part)))
    small = (
        (local_any.at[0, 0], own_side), (local_any.at[0, 1], far_side),
        (border_any.at[0], border_pick), (pick_any, face_pick), (facing_any, face_pair),
    )
    small = start_all(copies_of(small, small_sem))
    sends = []
    for part in range(parts):
        wait_all(large[part])
        build_table(verts, stiffness, table, part * rows, (part + 1) * rows)
    wait_all(small)

    @pl.loop(0, near.shape[0] // 8, unroll=16)
    def pairs(n):
        own, far = entry_at(table, own_side[n]), entry_at(table, far_side[n])
        near[pl.ds(pl.multiple_of(n * 8, 8), 8), :] = jnp.where(row < 4, own, far)

    sends += start_all(copies_of([(near, near_any)], out_sem))

    @pl.loop(0, border.shape[0] // 8, unroll=16)
    def borders(n):
        border[pl.ds(pl.multiple_of(n * 8, 8), 8), :] = entry_at(table, border_pick[n])

    sends += start_all(copies_of([(border, border_out)], out_sem, 3))
    @pl.loop(0, face_lo.shape[0] // 8, unroll=8)
    def face(k):
        for side, out in ((0, face_lo), (1, face_hi)):
            target = face_pair[0, side, k]
            level = jnp.where(target >= 0, 0.0, OFF)
            own = entry_at(table, jnp.maximum(target, 0)) + jnp.where(row == 3, level, 0.0)
            out[pl.ds(pl.multiple_of(k * 8, 8), 8), :] = jnp.where(row < 4, own, entry_at(table, face_pick[0, side, k]))

    sends += start_all(copies_of([(face_lo, lo_any), (face_hi, hi_any)], out_sem, 1))

    wait_all(sends)


def write_planes(force, planes, planes_out, sem, before=None):
    parts = sem.shape[0]
    rows = planes.shape[1] // parts
    sends = []
    for part in range(parts):

        @pl.loop(part * rows // 8, (part + 1) * rows // 8, unroll=32)
        def unpack(n):
            here = pl.ds(pl.multiple_of(n * 8, 8), 8)
            for c in range(3):
                value = force[pl.ds(n * 64 + c, 8, stride=8), :]
                planes[c, here, :] = value if before is None else planes[c, here, :] + value

        here = pl.ds(part * rows, rows)
        sends += start_all([pltpu.make_async_copy(planes.at[:, here, :], planes_out.at[:, here, :], sem.at[part])])
    wait_all(sends)


def local_kernel(
    local_any, near_any, after_any, planes_out, own_side, far_side, near, force, planes, sem, plane_sem, *scratch,
):
    row = row_index()
    pairs = own_side.shape[0]
    width = width_for(pairs)
    first = pl.ds(0, 2 * width * 8)
    rest = pl.ds(2 * width * 8, (pairs - 2 * width) * 8)
    copies = start_all(copies_of([(near_any.at[first], near.at[first])], sem))
    pieces = ((local_any.at[0, 0], own_side), (local_any.at[0, 1], far_side), (near_any.at[rest], near.at[rest]))
    others = start_all(copies_of(pieces, sem, 1))
    clear_rows(force)
    wait_all(copies)

    def load(n):
        entry = entry_at(near, n)
        own, far = split3(own_block(entry, row)), split3(far_block(entry, row))
        return (far, own), (own, far)

    def finish(n, push, react):
        entry = entry_at(near, n)
        add_at(force, own_side[n], push_of(entry, push))
        add_at(force, far_side[n], react_of(pltpu.roll(entry, 4, 0), react))

    run_tiles(0, pairs, width, load, finish, scratch, lambda: wait_all(others))
    write_planes(force, planes, planes_out, plane_sem)


def brick_kernel(border_any, message_any, back_any, react_any, border, message, back, react_out, index, sem, *scratch):
    row = row_index()
    count = message.shape[0]
    copies = [message_index(message_any, index, sem.at[2])]
    copies += copies_of(((border_any, border), (message_any, message)), sem)
    wait_all(start_all(copies))

    slots = count // lax.axis_size("brick")

    def far_entry(n):
        return entry_at(border, jnp.maximum(index[n, 0].astype(jnp.int32), 0))

    def load(n):
        n = slot_of(n, slots)
        x = jnp.concatenate([message[n], message[n]], axis=0)
        square = jnp.where(row < 3, x * x, 0.0)
        level = -0.5 * jnp.sum(square, axis=0, keepdims=True) + jnp.where(index[n, 0] >= 0.0, 0.0, OFF)
        own = split3(jnp.where(row == 3, level, jnp.where(row == 7, 1.0, x)))
        far = split3(far_block(far_entry(n), row))
        return (far, own), (own, far)

    def finish(n, push, react):
        n = slot_of(n, slots)
        back[n] = push_of(message[n], push[0:4])
        far = pltpu.roll(far_entry(n), 4, 0)
        react_out[pl.ds(pl.multiple_of(n * 8, 8), 8), :] = react_of(far, react)

    couples = count - slots
    run_tiles(0, couples, width_for(couples), load, finish, scratch)
    copies = [
        pltpu.make_async_copy(back, back_any, sem.at[0]),
        pltpu.make_async_copy(react_out, react_any, sem.at[1]),
    ]
    for copy in copies:
        copy.start()
    for copy in copies:
        copy.wait()


def face_kernel(
    border_any, pick_any, pair_any, asked_any, message, react_any, push_any, planes_in, sent_lo, sent_hi, got_lo, got_hi,
    planes_out, border_pick, face_pick, face_pair, recv_pair, brick_react, brick_push, planes, force, sent, got, index, sem, head_sem, plane_sem,
    *scratch,
):
    row = row_index()
    facing = face_pick.shape[2]
    width = width_for(facing)
    first = 2 * width * 8
    heads, copies = [], [message_index(message, index, sem.at[11])]
    for side, (mine, theirs) in enumerate(((sent_lo, got_lo), (sent_hi, got_hi))):
        base = side * facing * 8
        for n, (source, target) in enumerate(((mine, sent), (theirs, got))):
            head, rest = pl.ds(base, first), pl.ds(base + first, facing * 8 - first)
            heads.append(pltpu.make_async_copy(source.at[pl.ds(0, first)], target.at[head], head_sem.at[2 * side + n]))
            copies.append(
                pltpu.make_async_copy(source.at[pl.ds(first, facing * 8 - first)], target.at[rest], sem.at[2 * side + n])
            )
    for n, (source, target) in enumerate(
        (
            (border_any.at[0], border_pick), (pick_any, face_pick), (pair_any, face_pair), (react_any, brick_react),
            (asked_any, recv_pair), (push_any, brick_push),
        )
    ):
        copies.append(pltpu.make_async_copy(source, target, sem.at[n + 4]))
    before = pltpu.make_async_copy(planes_in, planes, sem.at[10])
    for copy in heads + copies + [before]:
        copy.start()
    clear_rows(force)
    wait_all(heads)

    layer = lax.axis_index("slab")
    has_low, has_high = layer > 0, layer < lax.axis_size("slab") - 1

    start = jnp.where(has_low, 0, facing)
    stop = jnp.where(has_high, 2 * facing, facing)
    bricks, slots = recv_pair.shape[1], recv_pair.shape[2]

    def add_brick(n):
        s = n + jnp.where(n >= lax.axis_index("brick"), 1, 0)
        for k in range(slots):
            slot = s * slots + k
            anchor = border_pick[jnp.maximum(index[slot, 0].astype(jnp.int32), 0)]
            add_at(force, anchor, entry_at(brick_react, slot))
            target = recv_pair[0, s, k]
            push = jnp.concatenate([brick_push[slot], jnp.zeros((4, 128), F32)], axis=0)
            add_at(force, jnp.maximum(target, 0), jnp.where(target >= 0, push, 0.0))

    def add_bricks():
        wait_all(copies)
        pl.loop(0, bricks - 1)(add_brick)

    def load(n):
        mine, theirs = entry_at(sent, n), entry_at(got, n)
        down = split3(far_block(theirs, row)), split3(own_block(theirs, row))
        return down, (split3(own_block(mine, row)), split3(far_block(mine, row)))

    def finish(n, push, react):
        side = (n >= facing).astype(jnp.int32)
        k = n - side * facing
        mine = entry_at(sent, n)
        add_at(force, jnp.maximum(face_pair[0, side, k], 0), push_of(mine, push))
        add_at(force, face_pick[0, side, k], react_of(pltpu.roll(mine, 4, 0), react))

    run_tiles(start, stop, width, load, finish, scratch, add_bricks)

    before.wait()
    write_planes(force, planes, planes_out, plane_sem, before)


HBM = pl.BlockSpec(memory_space=pltpu.HBM)


def call(kernel, out, in_specs, out_specs, scratch, cost):
    return pl.pallas_call(
        kernel,
        out_shape=out,
        in_specs=in_specs,
        out_specs=out_specs,
        scratch_shapes=scratch,
        compiler_params=pltpu.CompilerParams(vmem_limit_bytes=VMEM_LIMIT),
        cost_estimate=pl.CostEstimate(flops=cost[0], bytes_accessed=cost[1], transcendentals=cost[2]),
    )


def shape(*dims):
    return jax.ShapeDtypeStruct(dims, F32)


def body(verts, stiffness, local_pairs, border_pick, recv_src, recv_pair, face_pick, face_pair):
    patches = verts.shape[0]
    bricks, slots = recv_pair.shape[1], recv_pair.shape[2]
    facing = face_pick.shape[2]
    count = bricks * slots
    pairs = local_pairs.shape[2]
    layers = lax.axis_size("slab")
    tile = 128 * 128

    points = jnp.transpose(verts, (1, 0, 2))
    brick_msg = call(
        ask_kernel,
        shape(count, 4, 128),
        [HBM] * 3,
        HBM,
        scratch=[
            pltpu.SMEM(recv_src.shape, jnp.int32),
            pltpu.SMEM(recv_pair.shape, jnp.int32),
            pltpu.VMEM((3, patches, 128), F32),
            pltpu.VMEM((count, 4, 128), F32),
            pltpu.SemaphoreType.DMA((3,)),
        ],
        cost=(count * 512, patches * 128 * 12, 0),
    )(recv_src, recv_pair, points)
    arrived = lax.all_to_all(brick_msg, "brick", 0, 0, tiled=True)

    near, face_lo, face_hi, border = call(
        pack_kernel,
        (
            shape(pairs * 8, 128), shape(facing * 8, 128), shape(facing * 8, 128),
            shape(border_pick.shape[1] * 8, 128),
        ),
        [HBM] * 6,
        (HBM,) * 4,
        scratch=[pltpu.SMEM((pairs,), jnp.int32)] * 2
        + [pltpu.SMEM(dims, jnp.int32) for dims in (border_pick.shape[1:], face_pick.shape, face_pair.shape)]
        + [
            pltpu.VMEM((3, patches, 128), F32),
            pltpu.VMEM((patches, 128), F32),
            pltpu.VMEM((patches * 8, 128), F32),
            pltpu.VMEM((pairs * 8, 128), F32),
            pltpu.VMEM((facing * 8, 128), F32),
            pltpu.VMEM((facing * 8, 128), F32),
            pltpu.VMEM((border_pick.shape[1] * 8, 128), F32),
        ]
        + [pltpu.SemaphoreType.DMA((n,)) for n in (5, 8, 4)],
        cost=(patches * 128 * 60, patches * 128 * 48, 0),
    )(local_pairs, border_pick, face_pick, face_pair, points, stiffness)

    got_hi = lax.ppermute(face_lo, "slab", [((i + 1) % layers, i) for i in range(layers)])
    got_lo = lax.ppermute(face_hi, "slab", [(i, (i + 1) % layers) for i in range(layers)])

    back, brick_react = call(
        brick_kernel,
        (shape(count, 4, 128), shape(count * 8, 128)),
        [HBM, HBM],
        (HBM, HBM),
        scratch=[
            pltpu.VMEM(border.shape, F32),
            pltpu.VMEM(arrived.shape, F32),
            pltpu.VMEM((count, 4, 128), F32),
            pltpu.VMEM((count * 8, 128), F32),
            pltpu.SMEM((count, 128), F32),
            pltpu.SemaphoreType.DMA((3,)),
        ]
        + tile_scratch(WIDTH),
        cost=(count * tile * 400, patches * 128 * 32, count * tile),
    )(border, arrived)

    brick_push = lax.all_to_all(back, "brick", 0, 0, tiled=True)
    planes = call(
        local_kernel,
        shape(3, patches, 128),
        [HBM] * 3,
        HBM,
        scratch=[
            pltpu.SMEM((pairs,), jnp.int32),
            pltpu.SMEM((pairs,), jnp.int32),
            pltpu.VMEM((pairs * 8, 128), F32),
            pltpu.VMEM((patches * 8, 128), F32),
            pltpu.VMEM((3, patches, 128), F32),
            pltpu.SemaphoreType.DMA((4,)),
            pltpu.SemaphoreType.DMA((4,)),
        ]
        + tile_scratch(WIDTH),
        cost=(pairs * tile * 400, patches * 128 * 48, pairs * tile),
    )(local_pairs, near, back)

    out = call(
        face_kernel,
        shape(3, patches, 128),
        [HBM] * 12,
        HBM,
        scratch=[
            pltpu.SMEM(border_pick.shape[1:], jnp.int32),
            pltpu.SMEM(face_pick.shape, jnp.int32),
            pltpu.SMEM(face_pair.shape, jnp.int32),
            pltpu.SMEM(recv_pair.shape, jnp.int32),
            pltpu.VMEM((count * 8, 128), F32),
            pltpu.VMEM((count, 4, 128), F32),
            pltpu.VMEM((3, patches, 128), F32),
            pltpu.VMEM((patches * 8, 128), F32),
            pltpu.VMEM((2 * facing * 8, 128), F32),
            pltpu.VMEM((2 * facing * 8, 128), F32),
            pltpu.SMEM((count, 128), F32),
            pltpu.SemaphoreType.DMA((12,)),
            pltpu.SemaphoreType.DMA((4,)),
            pltpu.SemaphoreType.DMA((4,)),
        ]
        + tile_scratch(WIDTH),
        cost=(4 * facing * tile * 400, patches * 128 * 64, 4 * facing * tile),
    )(
        border_pick, face_pick, face_pair, recv_pair, arrived, brick_react, brick_push, planes,
        face_lo, face_hi, got_lo, got_hi,
    )
    return jnp.transpose(out, (1, 0, 2))


def solution(mesh):
    placed = (
        P(("slab", "brick"), None, None),
        P(("slab", "brick"), None),
        P(("slab", "brick"), None, None),
        P(("slab", "brick"), None),
        P(("slab", "brick"), None, None),
        P(("slab", "brick"), None, None),
        P(("slab", "brick"), None, None),
        P(("slab", "brick"), None, None),
    )
    return jax.shard_map(
        body,
        mesh=mesh,
        in_specs=placed,
        out_specs=P(("slab", "brick"), None, None),
        check_vma=False,
    )
```

```python
import math

import jax
import jax.numpy as jnp
from jax import lax
from jax.experimental import pallas as pl
from jax.experimental.pallas import tpu as pltpu
from jax.sharding import PartitionSpec as P

F32 = jnp.float32
BF16 = jnp.bfloat16
ALPHA = math.sqrt(math.log2(math.e))
PUSH = 1.0 / ALPHA
REACT = 1.0 / (3.0 * ALPHA)
OFF = -1.0e5
VMEM_LIMIT = 64 * 1024 * 1024
WIDTH = 8
MATMUL = (((1,), (0,)), ((), ()))


def row_index():
    return lax.broadcasted_iota(jnp.int32, (8, 128), 0)


def split3(x):
    high = x.astype(BF16).astype(F32)
    rest = x - high
    mid = rest.astype(BF16).astype(F32)
    return high, mid, rest - mid


def own_block(entry, row):
    return jnp.where(row < 4, entry, jnp.where(row == 7, 1.0, pltpu.roll(entry, 4, 0)))


def far_block(entry, row):
    return jnp.where(row < 3, pltpu.roll(entry, 4, 0), jnp.where(row == 3, 1.0, entry))


def own_rows(parts, row):
    high, mid, low = parts
    one = jnp.where(row == 7, 1.0, 0.0)
    return [high, mid + one, jnp.where(row < 3, high, low) + one]


def far_rows(parts, row):
    high, mid, low = parts
    copy = (row >= 4) & (row < 7)
    return [
        jnp.where(copy, mid, high),
        jnp.where(row < 4, high, mid),
        jnp.where((row >= 3) & (row < 7), high, low),
    ]


def entry_at(ref, index):
    return ref[pl.ds(pl.multiple_of(index * 8, 8), 8), :]


def add_at(ref, index, value):
    ref[pl.ds(pl.multiple_of(index * 8, 8), 8), :] += value


def spread(react):
    return react + pltpu.roll(react, 1, 1) + pltpu.roll(react, 2, 1)


def tile_scratch(width):
    return [
        pltpu.VMEM((2 * width, 128, 48), BF16),
        pltpu.VMEM((2 * width, 48, 256), BF16),
        pltpu.VMEM((2 * width, 32, 128), BF16),
        pltpu.VMEM((2 * width, 128, 256), BF16),
        pltpu.VMEM((2 * width, 128, 256), BF16),
        pltpu.VMEM((2 * width, 2, 8, 128), F32),
    ]


def run_tiles(start, stop, width, load, finish, scratch, filled=None, narrow=False):
    lefts, rights, thins, highs, lows, sums = scratch
    row = row_index()

    def prepare(n, slot):
        (far_down, own_down), (own_across, far_across) = load(n)
        left = far_rows(far_down, row) + own_rows(own_down, row)
        empty = [jnp.zeros((8, 128), F32)] * 3
        first = jnp.concatenate(own_rows(own_across, row) + empty, axis=0)
        second = jnp.concatenate(empty + far_rows(far_across, row), axis=0)
        lefts[slot] = jnp.concatenate(left, axis=0).astype(BF16).T
        rights[slot] = jnp.concatenate([first, second], axis=1).astype(BF16)
        thin = [far_down[0], far_down[1], own_down[0], own_down[1]]
        if narrow:
            thin_far = jnp.where(row < 4, far_down[0], jnp.where(row < 7, far_down[1], 0.0))
            thin_own = jnp.where(row >= 4, own_down[0], jnp.where(row < 3, own_down[1], 0.0))
            thin = [thin_far, thin_own]
        thins[slot, 0 : 8 * len(thin), :] = jnp.concatenate(thin, axis=0).astype(BF16)

    def energies(slot):
        energy = jnp.exp2(lax.dot_general(lefts[slot], rights[slot], MATMUL, preferred_element_type=F32))
        high = energy.astype(BF16)
        highs[slot] = high
        lows[slot] = (energy - high.astype(F32)).astype(BF16)

    def totals(slot):
        tall = jnp.concatenate([highs[slot], lows[slot]], axis=0)
        thin = thins[slot, 0 : 16 if narrow else 32, :]
        thin = jnp.concatenate([thin, thin], axis=1)
        result = lax.dot_general(thin, tall, MATMUL, preferred_element_type=F32)
        if narrow:
            push, react = result[0:8, 0:128], result[8:16, 128:256]
            push, react = push + pltpu.roll(push, 4, 0), react + pltpu.roll(react, 4, 0)
            return push, react
        push = result[0:8, 0:128] + result[8:16, 0:128]
        react = result[16:24, 128:256] + result[24:32, 128:256]
        return push, react

    last = stop - 1
    for q in range(2 * width):
        prepare(jnp.minimum(start + q, last), q)
    for q in range(width):
        energies(q)

    sums[width : 2 * width] = jnp.zeros((width, 2, 8, 128), F32)
    if filled is not None:
        filled()

    @pl.loop(0, (stop - start) // (2 * width))
    def step(m):
        base = start + m * (2 * width)
        for half in range(2):
            here, there = half * width, (1 - half) * width
            for q in range(width):
                finish(jnp.maximum(base + here + q - width, start), sums[there + q, 0], sums[there + q, 1])
                sums[here + q, 0], sums[here + q, 1] = totals(here + q)
                energies(there + q)
                prepare(jnp.minimum(base + 2 * width + here + q, last), here + q)

    for q in range(width):
        finish(stop - width + q, sums[width + q, 0], sums[width + q, 1])


def push_of(own, total):
    return (own * total[3:4] - total) * PUSH


def react_of(far, total):
    return spread((far * total[7:8] - total) * REACT)


def width_for(couples):
    return max(width for width in range(1, WIDTH + 1) if couples % (2 * width) == 0)


def build_table(verts, stiffness, table, first, last):
    @pl.loop(first // 8, last // 8, unroll=32)
    def build(step):
        base = pl.multiple_of(step * 8, 8)
        xs = [verts[c, pl.ds(base, 8), :] * ALPHA for c in range(3)]
        cs = [(x + pltpu.roll(x, 127, 1) + pltpu.roll(x, 126, 1)) * (1.0 / 3.0) for x in xs]
        strength = stiffness[pl.ds(base, 8), :]
        own = -0.5 * (xs[0] * xs[0] + xs[1] * xs[1] + xs[2] * xs[2])
        far = jnp.log2(strength) - 7.0 - 0.5 * (cs[0] * cs[0] + cs[1] * cs[1] + cs[2] * cs[2])
        for k, value in enumerate(xs + [own] + cs + [far]):
            table[pl.ds(step * 64 + k, 8, stride=8), :] = value


def clear_rows(ref):
    @pl.loop(0, ref.shape[0] // 64, unroll=8)
    def clear(n):
        ref[pl.ds(pl.multiple_of(n * 64, 64), 64), :] = jnp.zeros((64, 128), F32)


def slot_of(n, slots):
    return n + jnp.where(n >= lax.axis_index("brick") * slots, slots, 0)


def message_index(message, index, sem):
    return pltpu.make_async_copy(message.at[:, 3, :], index, sem)


def start_all(copies):
    for copy in copies:
        copy.start()
    return copies


def wait_all(copies):
    for copy in copies:
        copy.wait()


def copies_of(pairs, sem, first=0):
    return [pltpu.make_async_copy(source, target, sem.at[first + n]) for n, (source, target) in enumerate(pairs)]


def ask_kernel(src_any, pair_any, verts_any, brick_any, recv_src, recv_pair, verts, brick_msg, sem):
    wait_all(start_all(copies_of(((src_any, recv_src), (pair_any, recv_pair), (verts_any, verts)), sem)))
    bricks, slots = recv_pair.shape[1], recv_pair.shape[2]

    @pl.loop(0, bricks, unroll=4)
    def brick(s):
        for k in range(slots):
            target = recv_pair[0, s, k]
            wanted = jnp.where(target >= 0, recv_src[0, s, k], -1).astype(F32)
            place = pl.ds(jnp.maximum(target, 0), 1)
            for c in range(3):
                brick_msg[s * slots + k, c:c + 1] = verts[c, place, :] * ALPHA
            brick_msg[s * slots + k, 3:4] = jnp.full((1, 128), wanted, F32)

    wait_all(start_all(copies_of([(brick_msg, brick_any)], sem)))


def pack_kernel(
    local_any, border_any, pick_any, facing_any, verts_any, stiffness_any,
    near_any, lo_any, hi_any, border_out,
    own_side, far_side, border_pick, face_pick, face_pair, verts, stiffness, table, near,
    face_lo, face_hi, border, small_sem, large_sem, out_sem,
):
    patches = stiffness.shape[0]
    row = row_index()
    parts = large_sem.shape[0] // 2
    rows = patches // parts
    large = []
    for part in range(parts):
        here = pl.ds(part * rows, rows)
        pieces = ((verts_any.at[:, here, :], verts.at[:, here, :]), (stiffness_any.at[here], stiffness.at[here]))
        large.append(start_all(copies_of(pieces, large_sem, 2 * part)))
    small = (
        (local_any.at[0, 0], own_side), (local_any.at[0, 1], far_side),
        (border_any.at[0], border_pick), (pick_any, face_pick), (facing_any, face_pair),
    )
    small = start_all(copies_of(small, small_sem))
    sends = []
    for part in range(parts):
        wait_all(large[part])
        build_table(verts, stiffness, table, part * rows, (part + 1) * rows)
    wait_all(small)

    @pl.loop(0, near.shape[0] // 8, unroll=16)
    def pairs(n):
        own, far = entry_at(table, own_side[n]), entry_at(table, far_side[n])
        near[pl.ds(pl.multiple_of(n * 8, 8), 8), :] = jnp.where(row < 4, own, far)

    sends += start_all(copies_of([(near, near_any)], out_sem))

    @pl.loop(0, border.shape[0] // 8, unroll=16)
    def borders(n):
        border[pl.ds(pl.multiple_of(n * 8, 8), 8), :] = entry_at(table, border_pick[n])

    sends += start_all(copies_of([(border, border_out)], out_sem, 3))
    @pl.loop(0, face_lo.shape[0] // 8, unroll=8)
    def face(k):
        for side, out in ((0, face_lo), (1, face_hi)):
            target = face_pair[0, side, k]
            level = jnp.where(target >= 0, 0.0, OFF)
            own = entry_at(table, jnp.maximum(target, 0)) + jnp.where(row == 3, level, 0.0)
            out[pl.ds(pl.multiple_of(k * 8, 8), 8), :] = jnp.where(row < 4, own, entry_at(table, face_pick[0, side, k]))

    sends += start_all(copies_of([(face_lo, lo_any), (face_hi, hi_any)], out_sem, 1))

    wait_all(sends)


def write_planes(force, planes, planes_out, sem, before=None):
    parts = sem.shape[0]
    rows = planes.shape[1] // parts
    sends = []
    for part in range(parts):

        @pl.loop(part * rows // 8, (part + 1) * rows // 8, unroll=32)
        def unpack(n):
            here = pl.ds(pl.multiple_of(n * 8, 8), 8)
            for c in range(3):
                value = force[pl.ds(n * 64 + c, 8, stride=8), :]
                planes[c, here, :] = value if before is None else planes[c, here, :] + value

        here = pl.ds(part * rows, rows)
        sends += start_all([pltpu.make_async_copy(planes.at[:, here, :], planes_out.at[:, here, :], sem.at[part])])
    wait_all(sends)


def local_kernel(
    local_any, near_any, after_any, planes_out, own_side, far_side, near, force, planes, sem, plane_sem, *scratch,
):
    row = row_index()
    pairs = own_side.shape[0]
    width = width_for(pairs)
    first = pl.ds(0, 2 * width * 8)
    rest = pl.ds(2 * width * 8, (pairs - 2 * width) * 8)
    copies = start_all(copies_of([(near_any.at[first], near.at[first])], sem))
    pieces = ((local_any.at[0, 0], own_side), (local_any.at[0, 1], far_side), (near_any.at[rest], near.at[rest]))
    others = start_all(copies_of(pieces, sem, 1))
    clear_rows(force)
    wait_all(copies)

    def load(n):
        entry = entry_at(near, n)
        own, far = split3(own_block(entry, row)), split3(far_block(entry, row))
        return (far, own), (own, far)

    def finish(n, push, react):
        entry = entry_at(near, n)
        add_at(force, own_side[n], push_of(entry, push))
        add_at(force, far_side[n], react_of(pltpu.roll(entry, 4, 0), react))

    run_tiles(0, pairs, width, load, finish, scratch, lambda: wait_all(others))
    write_planes(force, planes, planes_out, plane_sem)


def brick_kernel(border_any, message_any, back_any, react_any, border, message, back, react_out, index, sem, *scratch):
    row = row_index()
    count = message.shape[0]
    copies = [message_index(message_any, index, sem.at[2])]
    copies += copies_of(((border_any, border), (message_any, message)), sem)
    wait_all(start_all(copies))

    slots = count // lax.axis_size("brick")

    def far_entry(n):
        return entry_at(border, jnp.maximum(index[n, 0].astype(jnp.int32), 0))

    def load(n):
        n = slot_of(n, slots)
        x = jnp.concatenate([message[n], message[n]], axis=0)
        square = jnp.where(row < 3, x * x, 0.0)
        level = -0.5 * jnp.sum(square, axis=0, keepdims=True) + jnp.where(index[n, 0] >= 0.0, 0.0, OFF)
        own = split3(jnp.where(row == 3, level, jnp.where(row == 7, 1.0, x)))
        far = split3(far_block(far_entry(n), row))
        return (far, own), (own, far)

    def finish(n, push, react):
        n = slot_of(n, slots)
        back[n] = push_of(message[n], push[0:4])
        far = pltpu.roll(far_entry(n), 4, 0)
        react_out[pl.ds(pl.multiple_of(n * 8, 8), 8), :] = react_of(far, react)

    couples = count - slots
    run_tiles(0, couples, width_for(couples), load, finish, scratch, narrow=True)
    copies = [
        pltpu.make_async_copy(back, back_any, sem.at[0]),
        pltpu.make_async_copy(react_out, react_any, sem.at[1]),
    ]
    for copy in copies:
        copy.start()
    for copy in copies:
        copy.wait()


def face_kernel(
    border_any, pick_any, pair_any, asked_any, message, react_any, push_any, planes_in, sent_lo, sent_hi, got_lo, got_hi,
    planes_out, border_pick, face_pick, face_pair, recv_pair, brick_react, brick_push, planes, force, sent, got, index, sem, head_sem, plane_sem,
    *scratch,
):
    row = row_index()
    facing = face_pick.shape[2]
    width = width_for(facing)
    first = 2 * width * 8
    heads, copies = [], [message_index(message, index, sem.at[11])]
    for side, (mine, theirs) in enumerate(((sent_lo, got_lo), (sent_hi, got_hi))):
        base = side * facing * 8
        for n, (source, target) in enumerate(((mine, sent), (theirs, got))):
            head, rest = pl.ds(base, first), pl.ds(base + first, facing * 8 - first)
            heads.append(pltpu.make_async_copy(source.at[pl.ds(0, first)], target.at[head], head_sem.at[2 * side + n]))
            copies.append(
                pltpu.make_async_copy(source.at[pl.ds(first, facing * 8 - first)], target.at[rest], sem.at[2 * side + n])
            )
    for n, (source, target) in enumerate(
        (
            (border_any.at[0], border_pick), (pick_any, face_pick), (pair_any, face_pair), (react_any, brick_react),
            (asked_any, recv_pair), (push_any, brick_push),
        )
    ):
        copies.append(pltpu.make_async_copy(source, target, sem.at[n + 4]))
    before = pltpu.make_async_copy(planes_in, planes, sem.at[10])
    for copy in heads + copies + [before]:
        copy.start()
    clear_rows(force)
    wait_all(heads)

    layer = lax.axis_index("slab")
    has_low, has_high = layer > 0, layer < lax.axis_size("slab") - 1

    start = jnp.where(has_low, 0, facing)
    stop = jnp.where(has_high, 2 * facing, facing)
    bricks, slots = recv_pair.shape[1], recv_pair.shape[2]

    def add_brick(n):
        s = n + jnp.where(n >= lax.axis_index("brick"), 1, 0)
        for k in range(slots):
            slot = s * slots + k
            anchor = border_pick[jnp.maximum(index[slot, 0].astype(jnp.int32), 0)]
            add_at(force, anchor, entry_at(brick_react, slot))
            target = recv_pair[0, s, k]
            push = jnp.concatenate([brick_push[slot], jnp.zeros((4, 128), F32)], axis=0)
            add_at(force, jnp.maximum(target, 0), jnp.where(target >= 0, push, 0.0))

    def add_bricks():
        wait_all(copies)
        pl.loop(0, bricks - 1)(add_brick)

    def load(n):
        mine, theirs = entry_at(sent, n), entry_at(got, n)
        down = split3(far_block(theirs, row)), split3(own_block(theirs, row))
        return down, (split3(own_block(mine, row)), split3(far_block(mine, row)))

    def finish(n, push, react):
        side = (n >= facing).astype(jnp.int32)
        k = n - side * facing
        mine = entry_at(sent, n)
        add_at(force, jnp.maximum(face_pair[0, side, k], 0), push_of(mine, push))
        add_at(force, face_pick[0, side, k], react_of(pltpu.roll(mine, 4, 0), react))

    run_tiles(start, stop, width, load, finish, scratch, add_bricks)

    before.wait()
    write_planes(force, planes, planes_out, plane_sem, before)


HBM = pl.BlockSpec(memory_space=pltpu.HBM)


def call(kernel, out, in_specs, out_specs, scratch, cost):
    return pl.pallas_call(
        kernel,
        out_shape=out,
        in_specs=in_specs,
        out_specs=out_specs,
        scratch_shapes=scratch,
        compiler_params=pltpu.CompilerParams(vmem_limit_bytes=VMEM_LIMIT),
        cost_estimate=pl.CostEstimate(flops=cost[0], bytes_accessed=cost[1], transcendentals=cost[2]),
    )


def shape(*dims):
    return jax.ShapeDtypeStruct(dims, F32)


def body(verts, stiffness, local_pairs, border_pick, recv_src, recv_pair, face_pick, face_pair):
    patches = verts.shape[0]
    bricks, slots = recv_pair.shape[1], recv_pair.shape[2]
    facing = face_pick.shape[2]
    count = bricks * slots
    pairs = local_pairs.shape[2]
    layers = lax.axis_size("slab")
    tile = 128 * 128

    points = jnp.transpose(verts, (1, 0, 2))
    brick_msg = call(
        ask_kernel,
        shape(count, 4, 128),
        [HBM] * 3,
        HBM,
        scratch=[
            pltpu.SMEM(recv_src.shape, jnp.int32),
            pltpu.SMEM(recv_pair.shape, jnp.int32),
            pltpu.VMEM((3, patches, 128), F32),
            pltpu.VMEM((count, 4, 128), F32),
            pltpu.SemaphoreType.DMA((3,)),
        ],
        cost=(count * 512, patches * 128 * 12, 0),
    )(recv_src, recv_pair, points)
    arrived = lax.all_to_all(brick_msg, "brick", 0, 0, tiled=True)

    near, face_lo, face_hi, border = call(
        pack_kernel,
        (
            shape(pairs * 8, 128), shape(facing * 8, 128), shape(facing * 8, 128),
            shape(border_pick.shape[1] * 8, 128),
        ),
        [HBM] * 6,
        (HBM,) * 4,
        scratch=[pltpu.SMEM((pairs,), jnp.int32)] * 2
        + [pltpu.SMEM(dims, jnp.int32) for dims in (border_pick.shape[1:], face_pick.shape, face_pair.shape)]
        + [
            pltpu.VMEM((3, patches, 128), F32),
            pltpu.VMEM((patches, 128), F32),
            pltpu.VMEM((patches * 8, 128), F32),
            pltpu.VMEM((pairs * 8, 128), F32),
            pltpu.VMEM((facing * 8, 128), F32),
            pltpu.VMEM((facing * 8, 128), F32),
            pltpu.VMEM((border_pick.shape[1] * 8, 128), F32),
        ]
        + [pltpu.SemaphoreType.DMA((n,)) for n in (5, 8, 4)],
        cost=(patches * 128 * 60, patches * 128 * 48, 0),
    )(local_pairs, border_pick, face_pick, face_pair, points, stiffness)

    got_hi = lax.ppermute(face_lo, "slab", [((i + 1) % layers, i) for i in range(layers)])
    got_lo = lax.ppermute(face_hi, "slab", [(i, (i + 1) % layers) for i in range(layers)])

    back, brick_react = call(
        brick_kernel,
        (shape(count, 4, 128), shape(count * 8, 128)),
        [HBM, HBM],
        (HBM, HBM),
        scratch=[
            pltpu.VMEM(border.shape, F32),
            pltpu.VMEM(arrived.shape, F32),
            pltpu.VMEM((count, 4, 128), F32),
            pltpu.VMEM((count * 8, 128), F32),
            pltpu.SMEM((count, 128), F32),
            pltpu.SemaphoreType.DMA((3,)),
        ]
        + tile_scratch(WIDTH),
        cost=(count * tile * 400, patches * 128 * 32, count * tile),
    )(border, arrived)

    brick_push = lax.all_to_all(back, "brick", 0, 0, tiled=True)
    planes = call(
        local_kernel,
        shape(3, patches, 128),
        [HBM] * 3,
        HBM,
        scratch=[
            pltpu.SMEM((pairs,), jnp.int32),
            pltpu.SMEM((pairs,), jnp.int32),
            pltpu.VMEM((pairs * 8, 128), F32),
            pltpu.VMEM((patches * 8, 128), F32),
            pltpu.VMEM((3, patches, 128), F32),
            pltpu.SemaphoreType.DMA((4,)),
            pltpu.SemaphoreType.DMA((4,)),
        ]
        + tile_scratch(WIDTH),
        cost=(pairs * tile * 400, patches * 128 * 48, pairs * tile),
    )(local_pairs, near, back)

    out = call(
        face_kernel,
        shape(3, patches, 128),
        [HBM] * 12,
        HBM,
        scratch=[
            pltpu.SMEM(border_pick.shape[1:], jnp.int32),
            pltpu.SMEM(face_pick.shape, jnp.int32),
            pltpu.SMEM(face_pair.shape, jnp.int32),
            pltpu.SMEM(recv_pair.shape, jnp.int32),
            pltpu.VMEM((count * 8, 128), F32),
            pltpu.VMEM((count, 4, 128), F32),
            pltpu.VMEM((3, patches, 128), F32),
            pltpu.VMEM((patches * 8, 128), F32),
            pltpu.VMEM((2 * facing * 8, 128), F32),
            pltpu.VMEM((2 * facing * 8, 128), F32),
            pltpu.SMEM((count, 128), F32),
            pltpu.SemaphoreType.DMA((12,)),
            pltpu.SemaphoreType.DMA((4,)),
            pltpu.SemaphoreType.DMA((4,)),
        ]
        + tile_scratch(WIDTH),
        cost=(4 * facing * tile * 400, patches * 128 * 64, 4 * facing * tile),
    )(
        border_pick, face_pick, face_pair, recv_pair, arrived, brick_react, brick_push, planes,
        face_lo, face_hi, got_lo, got_hi,
    )
    return jnp.transpose(out, (1, 0, 2))


def solution(mesh):
    placed = (
        P(("slab", "brick"), None, None),
        P(("slab", "brick"), None),
        P(("slab", "brick"), None, None),
        P(("slab", "brick"), None),
        P(("slab", "brick"), None, None),
        P(("slab", "brick"), None, None),
        P(("slab", "brick"), None, None),
        P(("slab", "brick"), None, None),
    )
    return jax.shard_map(
        body,
        mesh=mesh,
        in_specs=placed,
        out_specs=P(("slab", "brick"), None, None),
        check_vma=False,
    )
```

```python
import math

import jax
import jax.numpy as jnp
from jax import lax
from jax.experimental import pallas as pl
from jax.experimental.pallas import tpu as pltpu
from jax.sharding import PartitionSpec as P

F32 = jnp.float32
BF16 = jnp.bfloat16
ALPHA = math.sqrt(math.log2(math.e))
PUSH = 1.0 / ALPHA
REACT = 1.0 / (3.0 * ALPHA)
OFF = -1.0e5
VMEM_LIMIT = 64 * 1024 * 1024
WIDTH = 8
MATMUL = (((1,), (0,)), ((), ()))


def row_index():
    return lax.broadcasted_iota(jnp.int32, (8, 128), 0)


def split3(x):
    high = x.astype(BF16).astype(F32)
    rest = x - high
    mid = rest.astype(BF16).astype(F32)
    return high, mid, rest - mid


def own_block(entry, row):
    return jnp.where(row < 4, entry, jnp.where(row == 7, 1.0, pltpu.roll(entry, 4, 0)))


def far_block(entry, row):
    return jnp.where(row < 3, pltpu.roll(entry, 4, 0), jnp.where(row == 3, 1.0, entry))


def own_rows(parts, row):
    high, mid, low = parts
    one = jnp.where(row == 7, 1.0, 0.0)
    return [high, mid + one, jnp.where(row < 3, high, low) + one]


def far_rows(parts, row):
    high, mid, low = parts
    copy = (row >= 4) & (row < 7)
    return [
        jnp.where(copy, mid, high),
        jnp.where(row < 4, high, mid),
        jnp.where((row >= 3) & (row < 7), high, low),
    ]


def entry_at(ref, index):
    return ref[pl.ds(pl.multiple_of(index * 8, 8), 8), :]


def add_at(ref, index, value):
    ref[pl.ds(pl.multiple_of(index * 8, 8), 8), :] += value


def spread(react):
    return react + pltpu.roll(react, 1, 1) + pltpu.roll(react, 2, 1)


def tile_scratch(width):
    return [
        pltpu.VMEM((2 * width, 128, 48), BF16),
        pltpu.VMEM((2 * width, 48, 256), BF16),
        pltpu.VMEM((2 * width, 32, 128), BF16),
        pltpu.VMEM((2 * width, 128, 256), BF16),
        pltpu.VMEM((2 * width, 128, 256), BF16),
        pltpu.VMEM((2 * width, 2, 8, 128), F32),
    ]


def run_tiles(start, stop, width, load, finish, scratch, filled=None, narrow=False):
    lefts, rights, thins, highs, lows, sums = scratch
    row = row_index()

    def prepare(n, slot):
        (far_down, own_down), (own_across, far_across) = load(n)
        left = far_rows(far_down, row) + own_rows(own_down, row)
        empty = [jnp.zeros((8, 128), F32)] * 3
        first = jnp.concatenate(own_rows(own_across, row) + empty, axis=0)
        second = jnp.concatenate(empty + far_rows(far_across, row), axis=0)
        lefts[slot] = jnp.concatenate(left, axis=0).astype(BF16).T
        rights[slot] = jnp.concatenate([first, second], axis=1).astype(BF16)
        thin = [far_down[0], far_down[1], own_down[0], own_down[1]]
        if narrow:
            thin_far = jnp.where(row < 4, far_down[0], jnp.where(row < 7, far_down[1], 0.0))
            thin_own = jnp.where(row >= 4, own_down[0], jnp.where(row < 3, own_down[1], 0.0))
            thin = [thin_far, thin_own]
        thins[slot, 0 : 8 * len(thin), :] = jnp.concatenate(thin, axis=0).astype(BF16)

    def energies(slot):
        energy = jnp.exp2(lax.dot_general(lefts[slot], rights[slot], MATMUL, preferred_element_type=F32))
        high = energy.astype(BF16)
        highs[slot] = high
        lows[slot] = (energy - high.astype(F32)).astype(BF16)

    def totals(slot):
        tall = jnp.concatenate([highs[slot], lows[slot]], axis=0)
        thin = thins[slot, 0 : 16 if narrow else 32, :]
        thin = jnp.concatenate([thin, thin], axis=1)
        result = lax.dot_general(thin, tall, MATMUL, preferred_element_type=F32)
        if narrow:
            push, react = result[0:8, 0:128], result[8:16, 128:256]
            push, react = push + pltpu.roll(push, 4, 0), react + pltpu.roll(react, 4, 0)
            return push, react
        push = result[0:8, 0:128] + result[8:16, 0:128]
        react = result[16:24, 128:256] + result[24:32, 128:256]
        return push, react

    last = stop - 1
    for q in range(2 * width):
        prepare(jnp.minimum(start + q, last), q)
    for q in range(width):
        energies(q)

    sums[width : 2 * width] = jnp.zeros((width, 2, 8, 128), F32)
    if filled is not None:
        filled()

    @pl.loop(0, (stop - start) // (2 * width))
    def step(m):
        base = start + m * (2 * width)
        for half in range(2):
            here, there = half * width, (1 - half) * width
            for q in range(width):
                finish(jnp.maximum(base + here + q - width, start), sums[there + q, 0], sums[there + q, 1])
                sums[here + q, 0], sums[here + q, 1] = totals(here + q)
                energies(there + q)
                prepare(jnp.minimum(base + 2 * width + here + q, last), here + q)

    for q in range(width):
        finish(stop - width + q, sums[width + q, 0], sums[width + q, 1])


def push_of(own, total):
    return (own * total[3:4] - total) * PUSH


def react_of(far, total):
    return spread((far * total[7:8] - total) * REACT)


def width_for(couples):
    return max(width for width in range(1, WIDTH + 1) if couples % (2 * width) == 0)


def build_table(verts, stiffness, table, first, last):
    @pl.loop(first // 8, last // 8, unroll=32)
    def build(step):
        base = pl.multiple_of(step * 8, 8)
        xs = [verts[c, pl.ds(base, 8), :] * ALPHA for c in range(3)]
        cs = [(x + pltpu.roll(x, 127, 1) + pltpu.roll(x, 126, 1)) * (1.0 / 3.0) for x in xs]
        strength = stiffness[pl.ds(base, 8), :]
        own = -0.5 * (xs[0] * xs[0] + xs[1] * xs[1] + xs[2] * xs[2])
        far = jnp.log2(strength) - 7.0 - 0.5 * (cs[0] * cs[0] + cs[1] * cs[1] + cs[2] * cs[2])
        for k, value in enumerate(xs + [own] + cs + [far]):
            table[pl.ds(step * 64 + k, 8, stride=8), :] = value


def clear_rows(ref):
    @pl.loop(0, ref.shape[0] // 64, unroll=8)
    def clear(n):
        ref[pl.ds(pl.multiple_of(n * 64, 64), 64), :] = jnp.zeros((64, 128), F32)


def slot_of(n, slots):
    return n + jnp.where(n >= lax.axis_index("brick") * slots, slots, 0)


def message_index(message, index, sem):
    return pltpu.make_async_copy(message.at[:, 3, :], index, sem)


def start_all(copies):
    for copy in copies:
        copy.start()
    return copies


def wait_all(copies):
    for copy in copies:
        copy.wait()


def copies_of(pairs, sem, first=0):
    return [pltpu.make_async_copy(source, target, sem.at[first + n]) for n, (source, target) in enumerate(pairs)]


def ask_kernel(src_any, pair_any, verts_any, brick_any, recv_src, recv_pair, verts, brick_msg, sem):
    wait_all(start_all(copies_of(((src_any, recv_src), (pair_any, recv_pair), (verts_any, verts)), sem)))
    bricks, slots = recv_pair.shape[1], recv_pair.shape[2]

    @pl.loop(0, bricks, unroll=4)
    def brick(s):
        for k in range(slots):
            target = recv_pair[0, s, k]
            wanted = jnp.where(target >= 0, recv_src[0, s, k], -1).astype(F32)
            place = pl.ds(jnp.maximum(target, 0), 1)
            for c in range(3):
                brick_msg[s * slots + k, c:c + 1] = verts[c, place, :] * ALPHA
            brick_msg[s * slots + k, 3:4] = jnp.full((1, 128), wanted, F32)

    wait_all(start_all(copies_of([(brick_msg, brick_any)], sem)))


def pack_kernel(
    local_any, border_any, pick_any, facing_any, verts_any, stiffness_any,
    near_any, lo_any, hi_any, border_out,
    own_side, far_side, border_pick, face_pick, face_pair, verts, stiffness, table, near,
    face_lo, face_hi, border, small_sem, large_sem, out_sem,
):
    patches = stiffness.shape[0]
    row = row_index()
    parts = large_sem.shape[0] // 2
    rows = patches // parts
    large = []
    for part in range(parts):
        here = pl.ds(part * rows, rows)
        pieces = ((verts_any.at[:, here, :], verts.at[:, here, :]), (stiffness_any.at[here], stiffness.at[here]))
        large.append(start_all(copies_of(pieces, large_sem, 2 * part)))
    small = (
        (local_any.at[0, 0], own_side), (local_any.at[0, 1], far_side),
        (border_any.at[0], border_pick), (pick_any, face_pick), (facing_any, face_pair),
    )
    small = start_all(copies_of(small, small_sem))
    sends = []
    for part in range(parts):
        wait_all(large[part])
        build_table(verts, stiffness, table, part * rows, (part + 1) * rows)
    wait_all(small)

    @pl.loop(0, near.shape[0] // 8, unroll=16)
    def pairs(n):
        own, far = entry_at(table, own_side[n]), entry_at(table, far_side[n])
        near[pl.ds(pl.multiple_of(n * 8, 8), 8), :] = jnp.where(row < 4, own, far)

    sends += start_all(copies_of([(near, near_any)], out_sem))

    @pl.loop(0, border.shape[0] // 8, unroll=16)
    def borders(n):
        border[pl.ds(pl.multiple_of(n * 8, 8), 8), :] = entry_at(table, border_pick[n])

    sends += start_all(copies_of([(border, border_out)], out_sem, 3))
    @pl.loop(0, face_lo.shape[0] // 8, unroll=8)
    def face(k):
        for side, out in ((0, face_lo), (1, face_hi)):
            target = face_pair[0, side, k]
            level = jnp.where(target >= 0, 0.0, OFF)
            own = entry_at(table, jnp.maximum(target, 0)) + jnp.where(row == 3, level, 0.0)
            out[pl.ds(pl.multiple_of(k * 8, 8), 8), :] = jnp.where(row < 4, own, entry_at(table, face_pick[0, side, k]))

    sends += start_all(copies_of([(face_lo, lo_any), (face_hi, hi_any)], out_sem, 1))

    wait_all(sends)


def write_planes(force, planes, planes_out, sem, before=None):
    parts = sem.shape[0]
    rows = planes.shape[1] // parts
    sends = []
    for part in range(parts):

        @pl.loop(part * rows // 8, (part + 1) * rows // 8, unroll=16)
        def unpack(n):
            here = pl.ds(pl.multiple_of(n * 8, 8), 8)
            for c in range(3):
                value = force[pl.ds(n * 64 + c, 8, stride=8), :]
                planes[c, here, :] = value if before is None else planes[c, here, :] + value

        here = pl.ds(part * rows, rows)
        sends += start_all([pltpu.make_async_copy(planes.at[:, here, :], planes_out.at[:, here, :], sem.at[part])])
    wait_all(sends)


def local_kernel(
    local_any, near_any, after_any, planes_out, own_side, far_side, near, force, planes, sem, plane_sem, *scratch,
):
    row = row_index()
    pairs = own_side.shape[0]
    width = width_for(pairs)
    first = pl.ds(0, 2 * width * 8)
    rest = pl.ds(2 * width * 8, (pairs - 2 * width) * 8)
    copies = start_all(copies_of([(near_any.at[first], near.at[first])], sem))
    pieces = ((local_any.at[0, 0], own_side), (local_any.at[0, 1], far_side), (near_any.at[rest], near.at[rest]))
    others = start_all(copies_of(pieces, sem, 1))
    clear_rows(force)
    wait_all(copies)

    def load(n):
        entry = entry_at(near, n)
        own, far = split3(own_block(entry, row)), split3(far_block(entry, row))
        return (far, own), (own, far)

    def finish(n, push, react):
        entry = entry_at(near, n)
        add_at(force, own_side[n], push_of(entry, push))
        add_at(force, far_side[n], react_of(pltpu.roll(entry, 4, 0), react))

    run_tiles(0, pairs, width, load, finish, scratch, lambda: wait_all(others))
    write_planes(force, planes, planes_out, plane_sem)


def brick_kernel(border_any, message_any, back_any, react_any, border, message, back, react_out, index, sem, *scratch):
    row = row_index()
    count = message.shape[0]
    copies = [message_index(message_any, index, sem.at[2])]
    copies += copies_of(((border_any, border), (message_any, message)), sem)
    wait_all(start_all(copies))

    slots = count // lax.axis_size("brick")

    def far_entry(n):
        return entry_at(border, jnp.maximum(index[n, 0].astype(jnp.int32), 0))

    def load(n):
        n = slot_of(n, slots)
        x = jnp.concatenate([message[n], message[n]], axis=0)
        square = jnp.where(row < 3, x * x, 0.0)
        level = -0.5 * jnp.sum(square, axis=0, keepdims=True) + jnp.where(index[n, 0] >= 0.0, 0.0, OFF)
        own = split3(jnp.where(row == 3, level, jnp.where(row == 7, 1.0, x)))
        far = split3(far_block(far_entry(n), row))
        return (far, own), (own, far)

    def finish(n, push, react):
        n = slot_of(n, slots)
        back[n] = push_of(message[n], push[0:4])
        far = pltpu.roll(far_entry(n), 4, 0)
        react_out[pl.ds(pl.multiple_of(n * 8, 8), 8), :] = react_of(far, react)

    couples = count - slots
    run_tiles(0, couples, width_for(couples), load, finish, scratch, narrow=True)
    copies = [
        pltpu.make_async_copy(back, back_any, sem.at[0]),
        pltpu.make_async_copy(react_out, react_any, sem.at[1]),
    ]
    for copy in copies:
        copy.start()
    for copy in copies:
        copy.wait()


def face_kernel(
    border_any, pick_any, pair_any, asked_any, message, react_any, push_any, planes_in, sent_lo, sent_hi, got_lo, got_hi,
    planes_out, border_pick, face_pick, face_pair, recv_pair, brick_react, brick_push, planes, force, sent, got, index, sem, head_sem, plane_sem,
    *scratch,
):
    row = row_index()
    facing = face_pick.shape[2]
    width = width_for(facing)
    first = 2 * width * 8
    heads, copies = [], [message_index(message, index, sem.at[11])]
    for side, (mine, theirs) in enumerate(((sent_lo, got_lo), (sent_hi, got_hi))):
        base = side * facing * 8
        for n, (source, target) in enumerate(((mine, sent), (theirs, got))):
            head, rest = pl.ds(base, first), pl.ds(base + first, facing * 8 - first)
            heads.append(pltpu.make_async_copy(source.at[pl.ds(0, first)], target.at[head], head_sem.at[2 * side + n]))
            copies.append(
                pltpu.make_async_copy(source.at[pl.ds(first, facing * 8 - first)], target.at[rest], sem.at[2 * side + n])
            )
    for n, (source, target) in enumerate(
        (
            (border_any.at[0], border_pick), (pick_any, face_pick), (pair_any, face_pair), (react_any, brick_react),
            (asked_any, recv_pair), (push_any, brick_push),
        )
    ):
        copies.append(pltpu.make_async_copy(source, target, sem.at[n + 4]))
    before = pltpu.make_async_copy(planes_in, planes, sem.at[10])
    for copy in heads + copies + [before]:
        copy.start()
    clear_rows(force)
    wait_all(heads)

    layer = lax.axis_index("slab")
    has_low, has_high = layer > 0, layer < lax.axis_size("slab") - 1

    start = jnp.where(has_low, 0, facing)
    stop = jnp.where(has_high, 2 * facing, facing)
    bricks, slots = recv_pair.shape[1], recv_pair.shape[2]

    def add_brick(n):
        s = n + jnp.where(n >= lax.axis_index("brick"), 1, 0)
        for k in range(slots):
            slot = s * slots + k
            anchor = border_pick[jnp.maximum(index[slot, 0].astype(jnp.int32), 0)]
            add_at(force, anchor, entry_at(brick_react, slot))
            target = recv_pair[0, s, k]
            push = jnp.concatenate([brick_push[slot], jnp.zeros((4, 128), F32)], axis=0)
            add_at(force, jnp.maximum(target, 0), jnp.where(target >= 0, push, 0.0))

    def add_bricks():
        wait_all(copies)
        pl.loop(0, bricks - 1)(add_brick)

    def load(n):
        mine, theirs = entry_at(sent, n), entry_at(got, n)
        down = split3(far_block(theirs, row)), split3(own_block(theirs, row))
        return down, (split3(own_block(mine, row)), split3(far_block(mine, row)))

    def finish(n, push, react):
        side = (n >= facing).astype(jnp.int32)
        k = n - side * facing
        mine = entry_at(sent, n)
        add_at(force, jnp.maximum(face_pair[0, side, k], 0), push_of(mine, push))
        add_at(force, face_pick[0, side, k], react_of(pltpu.roll(mine, 4, 0), react))

    run_tiles(start, stop, width, load, finish, scratch, add_bricks)

    before.wait()
    write_planes(force, planes, planes_out, plane_sem, before)


HBM = pl.BlockSpec(memory_space=pltpu.HBM)


def call(kernel, out, in_specs, out_specs, scratch, cost):
    return pl.pallas_call(
        kernel,
        out_shape=out,
        in_specs=in_specs,
        out_specs=out_specs,
        scratch_shapes=scratch,
        compiler_params=pltpu.CompilerParams(vmem_limit_bytes=VMEM_LIMIT),
        cost_estimate=pl.CostEstimate(flops=cost[0], bytes_accessed=cost[1], transcendentals=cost[2]),
    )


def shape(*dims):
    return jax.ShapeDtypeStruct(dims, F32)


def body(verts, stiffness, local_pairs, border_pick, recv_src, recv_pair, face_pick, face_pair):
    patches = verts.shape[0]
    bricks, slots = recv_pair.shape[1], recv_pair.shape[2]
    facing = face_pick.shape[2]
    count = bricks * slots
    pairs = local_pairs.shape[2]
    layers = lax.axis_size("slab")
    tile = 128 * 128

    points = jnp.transpose(verts, (1, 0, 2))
    brick_msg = call(
        ask_kernel,
        shape(count, 4, 128),
        [HBM] * 3,
        HBM,
        scratch=[
            pltpu.SMEM(recv_src.shape, jnp.int32),
            pltpu.SMEM(recv_pair.shape, jnp.int32),
            pltpu.VMEM((3, patches, 128), F32),
            pltpu.VMEM((count, 4, 128), F32),
            pltpu.SemaphoreType.DMA((3,)),
        ],
        cost=(count * 512, patches * 128 * 12, 0),
    )(recv_src, recv_pair, points)
    arrived = lax.all_to_all(brick_msg, "brick", 0, 0, tiled=True)

    near, face_lo, face_hi, border = call(
        pack_kernel,
        (
            shape(pairs * 8, 128), shape(facing * 8, 128), shape(facing * 8, 128),
            shape(border_pick.shape[1] * 8, 128),
        ),
        [HBM] * 6,
        (HBM,) * 4,
        scratch=[pltpu.SMEM((pairs,), jnp.int32)] * 2
        + [pltpu.SMEM(dims, jnp.int32) for dims in (border_pick.shape[1:], face_pick.shape, face_pair.shape)]
        + [
            pltpu.VMEM((3, patches, 128), F32),
            pltpu.VMEM((patches, 128), F32),
            pltpu.VMEM((patches * 8, 128), F32),
            pltpu.VMEM((pairs * 8, 128), F32),
            pltpu.VMEM((facing * 8, 128), F32),
            pltpu.VMEM((facing * 8, 128), F32),
            pltpu.VMEM((border_pick.shape[1] * 8, 128), F32),
        ]
        + [pltpu.SemaphoreType.DMA((n,)) for n in (5, 8, 4)],
        cost=(patches * 128 * 60, patches * 128 * 48, 0),
    )(local_pairs, border_pick, face_pick, face_pair, points, stiffness)

    got_hi = lax.ppermute(face_lo, "slab", [((i + 1) % layers, i) for i in range(layers)])
    got_lo = lax.ppermute(face_hi, "slab", [(i, (i + 1) % layers) for i in range(layers)])

    back, brick_react = call(
        brick_kernel,
        (shape(count, 4, 128), shape(count * 8, 128)),
        [HBM, HBM],
        (HBM, HBM),
        scratch=[
            pltpu.VMEM(border.shape, F32),
            pltpu.VMEM(arrived.shape, F32),
            pltpu.VMEM((count, 4, 128), F32),
            pltpu.VMEM((count * 8, 128), F32),
            pltpu.SMEM((count, 128), F32),
            pltpu.SemaphoreType.DMA((3,)),
        ]
        + tile_scratch(WIDTH),
        cost=(count * tile * 400, patches * 128 * 32, count * tile),
    )(border, arrived)

    brick_push = lax.all_to_all(back, "brick", 0, 0, tiled=True)
    planes = call(
        local_kernel,
        shape(3, patches, 128),
        [HBM] * 3,
        HBM,
        scratch=[
            pltpu.SMEM((pairs,), jnp.int32),
            pltpu.SMEM((pairs,), jnp.int32),
            pltpu.VMEM((pairs * 8, 128), F32),
            pltpu.VMEM((patches * 8, 128), F32),
            pltpu.VMEM((3, patches, 128), F32),
            pltpu.SemaphoreType.DMA((4,)),
            pltpu.SemaphoreType.DMA((4,)),
        ]
        + tile_scratch(WIDTH),
        cost=(pairs * tile * 400, patches * 128 * 48, pairs * tile),
    )(local_pairs, near, back)

    out = call(
        face_kernel,
        shape(3, patches, 128),
        [HBM] * 12,
        HBM,
        scratch=[
            pltpu.SMEM(border_pick.shape[1:], jnp.int32),
            pltpu.SMEM(face_pick.shape, jnp.int32),
            pltpu.SMEM(face_pair.shape, jnp.int32),
            pltpu.SMEM(recv_pair.shape, jnp.int32),
            pltpu.VMEM((count * 8, 128), F32),
            pltpu.VMEM((count, 4, 128), F32),
            pltpu.VMEM((3, patches, 128), F32),
            pltpu.VMEM((patches * 8, 128), F32),
            pltpu.VMEM((2 * facing * 8, 128), F32),
            pltpu.VMEM((2 * facing * 8, 128), F32),
            pltpu.SMEM((count, 128), F32),
            pltpu.SemaphoreType.DMA((12,)),
            pltpu.SemaphoreType.DMA((4,)),
            pltpu.SemaphoreType.DMA((4,)),
        ]
        + tile_scratch(WIDTH),
        cost=(4 * facing * tile * 400, patches * 128 * 64, 4 * facing * tile),
    )(
        border_pick, face_pick, face_pair, recv_pair, arrived, brick_react, brick_push, planes,
        face_lo, face_hi, got_lo, got_hi,
    )
    return jnp.transpose(out, (1, 0, 2))


def solution(mesh):
    placed = (
        P(("slab", "brick"), None, None),
        P(("slab", "brick"), None),
        P(("slab", "brick"), None, None),
        P(("slab", "brick"), None),
        P(("slab", "brick"), None, None),
        P(("slab", "brick"), None, None),
        P(("slab", "brick"), None, None),
        P(("slab", "brick"), None, None),
    )
    return jax.shard_map(
        body,
        mesh=mesh,
        in_specs=placed,
        out_specs=P(("slab", "brick"), None, None),
        check_vma=False,
    )
```
